128 devices in a mesh: ctx: 16 (over x, z), tab: 8 (over y, core).
Axes of the slice: x: 4, y: 4, z: 4, core: 2. Of those that a mesh axis runs over, the one named last changes fastest.
Arguments:
- table: bfloat16 [16, 8, 4096, 512], P('ctx', 'tab'), may hold values from -6 to 6
- row_ids: int32 [16, 8, 256], P('ctx', 'tab'), may hold values from 0 to 4095
- dests: int32 [16, 8, 4], P('ctx'), may hold values from 0 to 7, as said below
- slots: int32 [16, 8, 4], P('ctx'), may hold values from 0 to 3, as said below
- lengths: int32 [8, 16], P('tab'), may hold values from 1 to 2048, 4096 in all within a row
- tile_mask: int32 [8, 64, 64], P('tab'), may hold values from 0 to 1, as said below
- w_in: bfloat16 [512, 2048], replicated, may hold values from -0.25 to 0.25
- w_out: bfloat16 [512, 512], replicated, may hold values from -0.25 to 0.25
- output_gradient: bfloat16 [8, 4096, 512], P('tab', 'ctx'), may hold values from -6 to 6
Outputs:
- layer_out: bfloat16 [8, 4096, 512], P('tab', 'ctx')
- table_grad: bfloat16 [16, 8, 4096, 512], P('ctx', 'tab')
The draws below stay inside these ranges and needn't reach their ends.
Inputs may be any that keep to these rules, and one draw needn't show every extreme that they name: `dests`: the 4 blocks of one device go to 4 different indices of tab, and every device of a ctx index receives exactly one block for each slot 0 to 3. `slots`: see dests. `lengths`: each row sums to 4096; its longest history has exactly 2048 positions. `tile_mask`: diagonal tiles are 1.
All inputs are finite; a program needn't handle non-finite values.
Results may differ from the reference program's by a relative error of at most 0.012.
Values may be sent and summed in bfloat16 or wider, within the bound.
No kernel may reach another device: no remote copies, remote signals or barrier semaphores. Data moves between devices by JAX's collectives and lax.ppermute only.
A program may use at most 192 MiB of HBM per device.

```python
import math
import jax
import jax.numpy as jnp
import numpy as np
from jax import lax

D = 512
H = 4
HD = 128
TAB_ROWS = 4096
BROWS = 64
NBLK = 4
NDOCS = 16
TOK = 256
LEN = 4096
MAXDOC = 2048
NTILE = 64
N_CTX = 16
N_TAB = 8


def routing(key):
    first, second, third = jax.random.split(key, 3)
    offsets = jax.vmap(lambda sub_key: jax.random.permutation(sub_key, N_TAB)[:NBLK])(jax.random.split(first, N_CTX))
    slot_order = jax.vmap(lambda sub_key: jax.random.permutation(sub_key, NBLK))(jax.random.split(second, N_CTX))
    block_order = jax.vmap(lambda sub_key: jax.random.permutation(sub_key, NBLK))(jax.random.split(third, N_CTX * N_TAB))
    block_order = block_order.reshape(N_CTX, N_TAB, NBLK).astype(jnp.int32)
    offset_table = jnp.broadcast_to(offsets[:, None, :].astype(jnp.int32), (N_CTX, N_TAB, NBLK))
    slot_table = jnp.broadcast_to(slot_order[:, None, :].astype(jnp.int32), (N_CTX, N_TAB, NBLK))
    chosen_offset = jnp.take_along_axis(offset_table, block_order, axis=2)
    chosen_slot = jnp.take_along_axis(slot_table, block_order, axis=2)
    sources = jnp.arange(N_TAB, dtype=jnp.int32)[None, :, None]
    destination = (sources + chosen_offset) % N_TAB
    return (destination.astype(jnp.int32), chosen_slot.astype(jnp.int32))


def draw_dests(key, part):
    return routing(key)[0]


def draw_slots(key, part):
    return routing(key)[1]


def draw_tile_mask(key, part):
    key = jax.random.fold_in(key, 7)
    coins = jax.random.randint(key, (N_TAB, NTILE, NTILE), 0, 5)
    diagonal = jnp.eye(NTILE, dtype=jnp.int32)[None, :, :]
    return jnp.maximum((coins < 3).astype(jnp.int32), diagonal).astype(jnp.int32)


def set_ends(values, stream_key, low, high):
    spot = [jax.random.randint(jax.random.fold_in(stream_key, axis), (), 0, length) for axis, length in enumerate(values.shape)]
    longest = values.shape.index(max(values.shape))
    next_to = spot[:longest] + [(spot[longest] + 1) % values.shape[longest]] + spot[longest + 1:]
    return values.at[tuple(spot)].set(low).at[tuple(next_to)].set(high)


def block_levels(rng, extent, cuts, low, largest):
    loudness, own = 1.0, jax.random.fold_in(rng, 6)
    for axis_at, shards_of in cuts:
        heights = jnp.exp(jax.random.uniform(jax.random.fold_in(own, axis_at), (shards_of,), jnp.float32, low / len(cuts), largest / len(cuts)))
        loudness = loudness * jnp.repeat(heights, extent[axis_at] // shards_of).reshape([-1 if axis == axis_at else 1 for axis in range(len(extent))])
    return loudness


def cumulative_ranks(number_of, lean):
    weights = [(1 << 20) // math.isqrt(standing ** lean) + 1 for standing in range(1, number_of + 1)]
    spread = 1 + sum(weights) // (1 << 30)
    return np.cumsum(np.array([max(1, weight // spread) for weight in weights]))


def ranked_ids(key, dims, amount, skew):
    listing = cumulative_ranks(amount, skew)
    lot = jax.random.randint(jax.random.fold_in(key, 1), dims, 0, int(listing[amount - 1]))
    standing = jnp.searchsorted(jnp.asarray(listing, jnp.int32), lot, side="right")
    return jax.random.permutation(jax.random.fold_in(key, 2), amount)[standing].astype(jnp.int32)


def profile(amount, total, most, lean):
    loads = [(1 << 20) // math.isqrt(rank ** lean) + 1 for rank in range(2, amount + 1)]
    spare, counts = total - most - (amount - 1), [1] * (amount - 1)
    while spare > 0:
        movable = [i for i in range(amount - 1) if counts[i] < most]
        whole, budget = sum([loads[i] for i in movable]), spare
        for i in movable:
            extra = min(most - counts[i], max(1, budget * loads[i] // whole), spare)
            counts[i] = counts[i] + extra
            spare = spare - extra
    return np.array([most] + counts)


def uneven_parts(key, amount, total, limit, skew):
    if amount == 2:
        one = jax.random.randint(key, (), max(1, total - limit), min(limit, total - 1) + 1)
        return jnp.stack([one, total - one])
    sizes = jnp.asarray(profile(amount, total, limit, skew), jnp.int32)
    pairs = (amount - 1) // 2
    giver, taker = sizes[1:1 + 2 * pairs:2], sizes[2:2 + 2 * pairs:2]
    margin = jnp.minimum(giver - 1, limit - taker)
    shifted = jax.random.randint(jax.random.fold_in(key, 1), (pairs,), 0, 1 << 20) % (margin + 1)
    sizes = sizes.at[1:1 + 2 * pairs:2].set(giver - shifted).at[2:2 + 2 * pairs:2].set(taker + shifted)
    return sizes[jax.random.permutation(jax.random.fold_in(key, 2), amount)]


def gaussian(stream_key, extent, width, bound, shards=(), held_as=jnp.bfloat16):
    drawn = width * jax.random.normal(stream_key, extent, jnp.float32)
    if shards:
        drawn = drawn * block_levels(stream_key, extent, shards, -0.22, 0.18)
    return jnp.clip(drawn, -bound, bound).astype(held_as)


def setup_inputs(seed: int = 0) -> dict:
    key_list = jax.random.split(jax.random.key(seed), 10)
    table = gaussian(key_list[0], (N_CTX, N_TAB, TAB_ROWS, D), 1.0, 6.0, ((0, 16), (1, 8)))
    row_ids = set_ends(ranked_ids(key_list[1], (N_CTX, N_TAB, TOK), TAB_ROWS, 1), jax.random.fold_in(key_list[1], 3), 0, TAB_ROWS - 1).astype(jnp.int32)
    dests = draw_dests(jax.random.fold_in(key_list[9], 71), 0)
    slots = draw_slots(jax.random.fold_in(key_list[9], 71), 0)
    lengths = jax.vmap(lambda own: uneven_parts(own, NDOCS, LEN, MAXDOC, 2))(jax.random.split(key_list[4], N_TAB)).reshape((N_TAB, NDOCS)).astype(jnp.int32)
    tile_mask = draw_tile_mask(jax.random.fold_in(key_list[9], 71), 0)
    w_in = gaussian(key_list[6], (D, 4 * D), D ** -0.5, 0.25)
    w_out = gaussian(key_list[7], (D, D), D ** -0.5, 0.25)
    output_gradient = gaussian(key_list[8], (N_TAB, LEN, D), 1.0, 6.0, ((0, 8), (1, 16)))
    return {"table": table, "row_ids": row_ids, "dests": dests, "slots": slots, "lengths": lengths, "tile_mask": tile_mask, "w_in": w_in, "w_out": w_out, "output_gradient": output_gradient}


epsilon = 1e-05

def layer_statistics(inputs):
    row_mean = lax.optimization_barrier(jnp.mean(inputs, axis=-1, keepdims=True))
    centred = inputs - row_mean
    inverse = lax.rsqrt(lax.optimization_barrier(jnp.mean(centred * centred, axis=-1, keepdims=True)) + epsilon)
    return (centred * inverse, inverse)

def norm_backward_pass(incoming_gradient, normalized_rows, inverse):
    first = lax.optimization_barrier(jnp.mean(incoming_gradient, axis=-1, keepdims=True))
    second = lax.optimization_barrier(jnp.mean(incoming_gradient * normalized_rows, axis=-1, keepdims=True))
    return inverse * (incoming_gradient - first - normalized_rows * second)

def silu_slope(argument):
    sigmoid_v = jax.nn.sigmoid(argument)
    return sigmoid_v * (1.0 + argument * (1.0 - sigmoid_v))

def rounded(argument):
    return lax.optimization_barrier(argument.astype(jnp.bfloat16)).astype(jnp.float32)

def position_of(stored, rows_dev, chain_count):
    half = rows_dev // 2
    owner = stored // rows_dev
    local = stored % rows_dev
    early = owner * half + local
    late = (2 * chain_count - 1 - owner) * half + local - half
    return jnp.where(local < half, early, late).astype(jnp.int32)

def doc_index(position, doc_ends):
    return lax.optimization_barrier(jnp.sum((position[:, None] >= doc_ends[None, :]).astype(jnp.int32), axis=1))

def allowed_pairs(query_pos, key_pos, doc_ends, tile_table):
    same_doc = doc_index(query_pos, doc_ends)[:, None] == doc_index(key_pos, doc_ends)[None, :]
    causal = key_pos[None, :] <= query_pos[:, None]
    tile_rows = jnp.take(tile_table, query_pos // BROWS, axis=0)
    tile_on = jnp.take(tile_rows, key_pos // BROWS, axis=1) > 0
    return (same_doc & causal & tile_on).astype(jnp.float32)

def group_layer(user_sequence, output_gradient, lengths, tile_table, w_in, w_out):
    score_scale = HD ** (-0.5)
    doc_ends = jnp.cumsum(lengths).astype(jnp.int32)
    centred_scaled_input, inverse_deviation = layer_statistics(user_sequence.astype(jnp.float32))
    normalized_rows = centred_scaled_input.astype(jnp.bfloat16)
    pre = jnp.dot(normalized_rows, w_in, preferred_element_type=jnp.float32)
    act = jax.nn.silu(pre).astype(jnp.bfloat16)
    up_part = act[:, 0:D].astype(jnp.float32)
    value_heads = act[:, D:2 * D].astype(jnp.float32).reshape(LEN, H, HD)
    query_all = act[:, 2 * D:3 * D].astype(jnp.float32)
    key_heads = act[:, 3 * D:4 * D].astype(jnp.float32).reshape(LEN, H, HD)
    key_pos = position_of(jnp.arange(LEN, dtype=jnp.int32), TOK, N_CTX)

    def forward_block(block_index):
        offset = block_index * TOK
        query_pos = position_of(offset + jnp.arange(TOK, dtype=jnp.int32), TOK, N_CTX)
        query_heads = lax.dynamic_slice_in_dim(query_all, offset, TOK, 0).reshape(TOK, H, HD)
        allowed = allowed_pairs(query_pos, key_pos, doc_ends, tile_table)
        scores = jnp.einsum('qhd,khd->hqk', query_heads, key_heads) * score_scale
        probs = rounded(jax.nn.silu(scores) * allowed[None])
        return jnp.einsum('hqk,khd->qhd', probs, value_heads).reshape(TOK, D)
    attn = lax.map(forward_block, jnp.arange(N_CTX, dtype=jnp.int32)).reshape(LEN, D)
    attn_hat, attn_inverse = layer_statistics(attn)
    mixed = (attn_hat * up_part).astype(jnp.bfloat16)
    layer_out = (user_sequence.astype(jnp.float32) + jnp.dot(mixed, w_out, preferred_element_type=jnp.float32)).astype(jnp.bfloat16)
    dmixed = jnp.dot(output_gradient, w_out.T, preferred_element_type=jnp.float32)
    d_up = dmixed * attn_hat
    d_attn = norm_backward_pass(dmixed * up_part, attn_hat, attn_inverse).astype(jnp.bfloat16).astype(jnp.float32)

    def backward_block(running, block_index):
        key_sum, value_sum = running
        offset = block_index * TOK
        query_pos = position_of(offset + jnp.arange(TOK, dtype=jnp.int32), TOK, N_CTX)
        query_heads = lax.dynamic_slice_in_dim(query_all, offset, TOK, 0).reshape(TOK, H, HD)
        grad_heads = lax.dynamic_slice_in_dim(d_attn, offset, TOK, 0).reshape(TOK, H, HD)
        allowed = allowed_pairs(query_pos, key_pos, doc_ends, tile_table)[None]
        scores = jnp.einsum('qhd,khd->hqk', query_heads, key_heads) * score_scale
        probs = rounded(jax.nn.silu(scores) * allowed)
        d_probs = jnp.einsum('qhd,khd->hqk', grad_heads, value_heads)
        d_scores = rounded(d_probs * silu_slope(scores) * allowed * score_scale)
        d_query = jnp.einsum('hqk,khd->qhd', d_scores, key_heads).reshape(TOK, D)
        key_sum = key_sum + jnp.einsum('hqk,qhd->khd', d_scores, query_heads).reshape(LEN, D)
        value_sum = value_sum + jnp.einsum('hqk,qhd->khd', probs, grad_heads).reshape(LEN, D)
        return ((key_sum, value_sum), d_query)
    zero_keys = jnp.zeros((LEN, D), jnp.float32)
    (d_key, d_value), d_query = lax.scan(backward_block, (zero_keys, zero_keys), jnp.arange(N_CTX, dtype=jnp.int32))
    d_query = d_query.reshape(LEN, D)
    d_act = jnp.concatenate([d_up, d_value, d_query, d_key], axis=1)
    d_pre = (d_act * silu_slope(pre)).astype(jnp.bfloat16)
    normalized_gradient = jnp.dot(d_pre, w_in.T, preferred_element_type=jnp.float32)
    sequence_gradient = (output_gradient.astype(jnp.float32) + norm_backward_pass(normalized_gradient, centred_scaled_input, inverse_deviation)).astype(jnp.bfloat16)
    return (layer_out, sequence_gradient)

def reference(table, row_ids, dests, slots, lengths, tile_mask, w_in, w_out, output_gradient):
    looked = jax.vmap(jax.vmap(lambda shard_rows, shard_ids: jnp.take(shard_rows, shard_ids, axis=0)))(table, row_ids)
    blocks = looked.reshape(N_CTX, N_TAB, NBLK, BROWS, D)
    ctx_index = jnp.broadcast_to(jnp.arange(N_CTX, dtype=jnp.int32)[:, None, None], dests.shape)
    placed = jnp.zeros((N_TAB, N_CTX, NBLK, BROWS, D), table.dtype).at[dests, ctx_index, slots].set(blocks)
    user_sequence = placed.reshape(N_TAB, LEN, D)

    def one_group(group_args):
        return group_layer(group_args[0], group_args[1], group_args[2], group_args[3], w_in, w_out)
    layer_out, sequence_gradient = lax.map(one_group, (user_sequence, output_gradient, lengths, tile_mask))
    returned = sequence_gradient.reshape(N_TAB, N_CTX, NBLK, BROWS, D)[dests, ctx_index, slots]
    returned = returned.reshape(N_CTX * N_TAB, TOK, D)
    flat_ids = row_ids.reshape(N_CTX * N_TAB, TOK)

    def table_rows(pair_args):
        grads, shard_ids = pair_args
        summed = jnp.zeros((TAB_ROWS, D), jnp.float32).at[shard_ids].add(grads.astype(jnp.float32))
        return summed.astype(jnp.bfloat16)
    table_grad = lax.map(table_rows, (returned, flat_ids)).reshape(N_CTX, N_TAB, TAB_ROWS, D)
    return (layer_out, table_grad)
```

```python
import functools

import jax
import jax.numpy as jnp
from jax import lax
from jax.experimental import pallas as pl
from jax.experimental.pallas import tpu as pltpu
from jax.sharding import Mesh, PartitionSpec as P

HEADS = 4
BROWS = 64
NBLK = 4
WIDTH = 512
HD = 128
ROWS = 256
CHUNK = 128
LENGTH = 4096
EPS = 1e-05
BF = jnp.bfloat16
F32 = jnp.float32
AXES = ("x", "z", "y", "c")
FAR = 1e9
KEY_TILE = 256
SCALE = HD ** (-0.5)


def device_id(x, z, y, c):
    return ((x * 4 + z) * 4 + y) * 2 + c


def all_coords():
    return [(x, z, y, c) for x in range(4) for z in range(4) for y in range(4) for c in range(2)]


def tab_pairs(step):
    out = []
    for x, z, y, c in all_coords():
        y2, c2 = divmod((y * 2 + c + step) % 8, 2)
        out.append((device_id(x, z, y, c), device_id(x, z, y2, c2)))
    return out


def main_pairs(j):
    return [
        (device_id(x, z, y, c), device_id((x + j) % 4, 2 * c + (z >> 1), y, z & 1))
        for x, z, y, c in all_coords()
    ]


def other_pairs(j):
    return [
        (device_id(x, z, y, c), device_id((x + j) % 4, 2 * c + 1 - (z >> 1), y, z & 1))
        for x, z, y, c in all_coords()
    ]


def core_pairs():
    return [(device_id(x, z, y, c), device_id(x, z, y, 1 - c)) for x, z, y, c in all_coords()]


def head_pairs(k):
    return [(device_id(x, z, y, c), device_id((x + k) % 4, z, y, c)) for x, z, y, c in all_coords()]


def back(pairs):
    return [(b, a) for a, b in pairs]


def send(value, pairs):
    return lax.ppermute(value, AXES, pairs)


def dot(a, b):
    return jnp.dot(a, b, preferred_element_type=F32)


def dot_nt(a, b):
    return lax.dot_general(a, b, (((1,), (1,)), ((), ())), preferred_element_type=F32)


def silu(z):
    h = 0.5 * z
    return h + h * jnp.tanh(h)


def silu_slope(z):
    h = 0.5 * z
    t = jnp.tanh(h)
    return 0.5 * (1.0 + t) * (1.0 + h * (1.0 - t))


def row_statistics(x):
    mean = jnp.mean(x, axis=-1, keepdims=True)
    centred = x - mean
    inverse = lax.rsqrt(jnp.mean(centred * centred, axis=-1, keepdims=True) + EPS)
    return centred * inverse, inverse


def norm_backward(grad, hat, inverse):
    first = jnp.mean(grad, axis=-1, keepdims=True)
    second = jnp.mean(grad * hat, axis=-1, keepdims=True)
    return inverse * (grad - first - hat * second)


def column_of(row):
    return jnp.transpose(jnp.broadcast_to(row, (CHUNK, CHUNK)))


def ds(start, size):
    return pl.ds(pl.multiple_of(start, size), size)


VMEM = pl.BlockSpec(memory_space=pltpu.VMEM)
SMEM = pl.BlockSpec(memory_space=pltpu.SMEM)


def shape(dims, dtype):
    return jax.ShapeDtypeStruct(dims, dtype)


def call(kernel, ins, specs, outs, scratch=(), flops=0, name=None):
    moved = sum(a.size * a.dtype.itemsize for a in ins)
    moved += sum(o.size * jnp.dtype(o.dtype).itemsize for o in outs)
    return pl.pallas_call(
        kernel,
        out_shape=outs,
        in_specs=specs,
        out_specs=[VMEM] * len(outs),
        scratch_shapes=list(scratch),
        compiler_params=pltpu.CompilerParams(vmem_limit_bytes=40 * 1024 * 1024),
        cost_estimate=pl.CostEstimate(flops=flops, bytes_accessed=moved, transcendentals=0),
        name=name,
    )(*ins)


def lookup_kernel(meta, dest, ids_ref, table_ref, *rest):
    outs, (total, column) = rest[:8], rest[8:]
    step = pl.program_id(0)
    tile = table_ref.shape[2]

    @pl.when(step == 0)
    def _():
        for k in range(8):
            outs[k][...] = jnp.zeros_like(outs[k])
        total[...] = jnp.zeros_like(total)
        for b in range(2):
            column[b * CHUNK : (b + 1) * CHUNK, :] = column_of(ids_ref[b : b + 1, :].astype(F32))

    lane = lax.broadcasted_iota(jnp.int32, (ROWS, CHUNK), 1).astype(F32)
    base = (step * tile).astype(F32)
    wanted = column[...] - base
    hits = [jnp.where(wanted == lane + float(n * CHUNK), 1.0, 0.0).astype(BF) for n in range(tile // CHUNK)]
    total[...] += dot(jnp.concatenate(hits, axis=1), table_ref[0, 0])

    @pl.when(step == pl.num_programs(0) - 1)
    def _():
        own = meta[2] * 2 + meta[3]
        for k in range(8):
            for p in range(NBLK):

                @pl.when(dest[own * NBLK + p] == lax.rem(own + k, 8))
                def _():
                    outs[k][...] = total[p * BROWS : (p + 1) * BROWS, :].astype(BF)


def prepare_kernel(meta, len_own, len_swap, mask_own, mask_swap, incoming, w_out, bounds, starts, key_pos, query_pos, dmixed):
    same = (meta[1] >> 1) == meta[3]
    chunk = lax.broadcasted_iota(jnp.int32, (32, CHUNK), 0)
    position = chunk * CHUNK + lax.broadcasted_iota(jnp.int32, (32, CHUNK), 1)
    lane = lax.broadcasted_iota(jnp.int32, (8, CHUNK), 1)
    row = lax.broadcasted_iota(jnp.int32, (8, CHUNK), 0)
    first, last = lane * CHUNK, lane * CHUNK + CHUNK - 1
    start = jnp.zeros((32, CHUNK), jnp.int32)
    chunk_start = jnp.zeros((8, CHUNK), jnp.int32)
    chunk_stop = jnp.full((8, CHUNK), LENGTH, jnp.int32)
    end = jnp.int32(0)
    for d in range(len_own.shape[0]):
        end = end + jnp.where(same, len_own[d], len_swap[d])
        start = jnp.where(position >= end, end, start)
        chunk_start = jnp.where(first >= end, end, chunk_start)
        chunk_stop = jnp.where(last < end, jnp.minimum(chunk_stop, end), chunk_stop)
    starts[...] = start.astype(F32)
    bounds[...] = jnp.where(row == 0, chunk_start, chunk_stop - 1)
    mask = jnp.where(same, mask_own[...], mask_swap[...]).astype(F32)
    turned = jnp.transpose(mask).astype(BF)
    mask = mask.astype(BF)
    for n in range(8):
        cols = slice(n * WIDTH, (n + 1) * WIDTH)
        spot = lax.broadcasted_iota(jnp.int32, (BROWS, WIDTH), 1) + n * WIDTH
        pick = jnp.where(
            lax.broadcasted_iota(jnp.int32, (BROWS, WIDTH), 0) == spot // BROWS, 1.0, 0.0
        ).astype(BF)
        spot = spot.astype(F32)
        key_pos[:, cols] = jnp.where(dot(mask, pick) > 0.5, spot, FAR)
        query_pos[:, cols] = jnp.where(dot(turned, pick) > 0.5, spot, -1.0)
    dmixed[...] = dot_nt(incoming[...], w_out[...])


def project_kernel(meta, dest, slot, *rest):
    blocks, (w_ref, dmixed_ref), rest = rest[:8], rest[8:10], rest[10:]
    hist, pre = rest[:2]
    main, other, extra = rest[2:6], rest[6:10], rest[10:14]
    act, grads = rest[14:]
    own = meta[2] * 2 + meta[3]
    for k in range(8):
        source = lax.rem(own - k + 8, 8)
        for p in range(NBLK):

            @pl.when(dest[source * NBLK + p] == own)
            def _():
                hist[ds(slot[source * NBLK + p] * BROWS, BROWS), :] = blocks[k][...]

    hat, _ = row_statistics(hist[...].astype(F32))
    normed = hat.astype(BF)
    for n in range(4):
        cols = slice(n * WIDTH, (n + 1) * WIDTH)
        part = dot(normed, w_ref[:, cols])
        pre[:, cols] = part
        act[:, cols] = silu(part).astype(BF)
    grads[...] = (dmixed_ref[...] * act[:, 0:WIDTH].astype(F32)).astype(BF)
    for j in range(4):
        head = lax.rem(meta[0] + j, 4) * HD
        key = act[:, ds(3 * WIDTH + head, HD)]
        value = act[:, ds(WIDTH + head, HD)]
        main[j][:, 0:HD] = key
        main[j][:, HD : 2 * HD] = value
        main[j][:, 2 * HD : 3 * HD] = act[:, ds(2 * WIDTH + head, HD)]
        other[j][:, 0:HD] = key
        other[j][:, HD : 2 * HD] = value
        extra[j][...] = grads[:, ds(head, HD)]


def place(meta):
    return meta[0], meta[1] & 1, meta[3]


def chunk_of(t, z):
    return 4 * t + jnp.where(t < 4, z, 3 - z)


def valid_keys(starts, key_pos, i, tile):
    pos = lax.broadcasted_iota(jnp.int32, (CHUNK, CHUNK), 0).astype(F32) + (i * CHUNK).astype(F32)
    start = column_of(starts[pl.ds(i, 1), :])
    repeat = KEY_TILE // CHUNK
    pos = jnp.concatenate([pos] * repeat, axis=1)
    start = jnp.concatenate([start] * repeat, axis=1)

    def at(tile):
        halves = [
            jnp.broadcast_to(key_pos[pl.ds(2 * i + n, 1), ds(tile * KEY_TILE, KEY_TILE)], (BROWS, KEY_TILE))
            for n in range(2)
        ]
        key = jnp.concatenate(halves, axis=0)
        return (key >= start) & (key <= pos)

    return at


def forward_kernel(meta, bounds, starts, key_pos, *rest):
    main, other, smain, sother, extra = (rest[4 * n : 4 * n + 4] for n in range(5))
    keys, queries, grads, attn = rest[20:24]
    returned, stats = rest[24:28], rest[28]
    head, r, core = place(meta)
    mine = 2 * r + core
    for j in range(4):
        x = lax.rem(head - j + 4, 4)
        for ref, z in (
            (main[j], mine),
            (other[j], 2 * (1 - r) + core),
            (smain[j], 2 * r + 1 - core),
            (sother[j], 2 * (1 - r) + 1 - core),
        ):
            c = 4 * x + z
            keys[ds(c * CHUNK, CHUNK), :] = ref[0:CHUNK, 0 : 2 * HD]
            keys[ds((31 - c) * CHUNK, CHUNK), :] = ref[CHUNK:ROWS, 0 : 2 * HD]
        for low, t in ((0, x), (CHUNK, 7 - x)):
            queries[ds(t * CHUNK, CHUNK), :] = main[j][low : low + CHUNK, 2 * HD : 3 * HD]
            grads[ds(t * CHUNK, CHUNK), :] = extra[j][low : low + CHUNK, :]

    def chunk(t, carry):
        i = chunk_of(t, mine)
        allowed = valid_keys(starts, key_pos, i, KEY_TILE)
        q = queries[ds(t * CHUNK, CHUNK), :]

        def step(n, total):
            rows = ds(n * KEY_TILE, KEY_TILE)
            h = dot_nt(q, keys[rows, 0:HD]) * (0.5 * SCALE)
            probs = jnp.where(allowed(n), h + h * jnp.tanh(h), 0.0).astype(BF)
            return total + dot(probs, keys[rows, HD : 2 * HD])

        first = bounds[0, i] // KEY_TILE
        last = (i * CHUNK + CHUNK - 1) // KEY_TILE
        total = lax.fori_loop(first, last + 1, step, jnp.zeros((CHUNK, HD), F32))
        rows = ds(t * CHUNK, CHUNK)
        attn[rows, :] = total
        e = grads[rows, :].astype(F32)
        mean = jnp.mean(total, axis=1, keepdims=True)
        centred = total - mean
        lane = lax.broadcasted_iota(jnp.int32, (CHUNK, CHUNK), 1)
        packed = jnp.where(lane == 0, mean, 0.0)
        packed = jnp.where(lane == 1, jnp.sum(centred * centred, axis=1, keepdims=True), packed)
        packed = jnp.where(lane == 2, jnp.sum(e, axis=1, keepdims=True), packed)
        packed = jnp.where(lane == 3, jnp.sum(e * centred, axis=1, keepdims=True), packed)
        stats[:, rows] = jnp.transpose(packed)[0:8, :]
        return carry

    lax.fori_loop(0, 8, chunk, 0)
    for j in range(4):
        x = lax.rem(head - j + 4, 4)
        for low, t in ((0, x), (CHUNK, 7 - x)):
            returned[j][low : low + CHUNK, :] = attn[ds(t * CHUNK, CHUNK), :].astype(BF)


def attn_grad_kernel(s0, s1, s2, s3, attn, grads, out):
    parts = [s[...] for s in (s0, s1, s2, s3)]
    means = [s[0:1, :] for s in parts]
    mean = (means[0] + means[1] + means[2] + means[3]) * 0.25
    spread = sum(s[1:2, :] + HD * (m - mean) * (m - mean) for s, m in zip(parts, means))
    inverse = lax.rsqrt(spread * (1.0 / WIDTH) + EPS)
    e_mean = sum(s[2:3, :] for s in parts) * (1.0 / WIDTH)
    e_on = sum(s[3:4, :] + (m - mean) * s[2:3, :] for s, m in zip(parts, means))
    e_on = e_on * inverse * (1.0 / WIDTH)
    for t in range(8):
        rows = slice(t * CHUNK, (t + 1) * CHUNK)
        cols = [column_of(v[:, rows]) for v in (mean, inverse, e_mean, e_on)]
        hat = (attn[rows, :] - cols[0]) * cols[1]
        out[rows, :] = (cols[1] * (grads[rows, :].astype(F32) - cols[2] - hat * cols[3])).astype(BF)


def query_grad_kernel(meta, bounds, starts, key_pos, keys, queries, d_attn, *rest):
    outs, total_ref = rest[:4], rest[4]
    head, r, core = place(meta)
    mine = 2 * r + core

    def chunk(t, carry):
        i = chunk_of(t, mine)
        allowed = valid_keys(starts, key_pos, i, KEY_TILE)
        rows_q = ds(t * CHUNK, CHUNK)
        q = queries[rows_q, :]
        g = d_attn[rows_q, :]

        def step(n, total):
            rows = ds(n * KEY_TILE, KEY_TILE)
            k = keys[rows, 0:HD]
            h = dot_nt(q, k) * (0.5 * SCALE)
            dp = dot_nt(g, keys[rows, HD : 2 * HD])
            th = jnp.tanh(h)
            d_scores = jnp.where(allowed(n), dp * ((1.0 + th) * (1.0 + h - h * th)), 0.0)
            return total + dot(d_scores.astype(BF), k)

        first = bounds[0, i] // KEY_TILE
        last = (i * CHUNK + CHUNK - 1) // KEY_TILE
        total = lax.fori_loop(first, last + 1, step, jnp.zeros((CHUNK, HD), F32))
        total_ref[rows_q, :] = (total * (0.5 * SCALE)).astype(BF)
        return carry

    lax.fori_loop(0, 8, chunk, 0)
    for j in range(4):
        x = lax.rem(head - j + 4, 4)
        for low, t in ((0, x), (CHUNK, 7 - x)):
            outs[j][low : low + CHUNK, :] = total_ref[ds(t * CHUNK, CHUNK), :]


def key_grad_kernel(meta, bounds, starts, query_pos, *rest):
    main, other, smain = (rest[4 * n : 4 * n + 4] for n in range(3))
    d_own, d_swap = rest[12:14]
    out_main, out_other = rest[14:18], rest[18:22]
    keys, both, sums = rest[22:25]
    head, r, core = place(meta)
    for j in range(4):
        x = lax.rem(head - j + 4, 4)
        for low, t in ((0, x), (CHUNK, 7 - x)):
            for ref, grad, half in ((main[j], d_own, core), (smain[j], d_swap, 1 - core)):
                side = half if low == 0 else 1 - half
                rows = ds((2 * t + side) * CHUNK, CHUNK)
                both[rows, 0:HD] = ref[low : low + CHUNK, 2 * HD : 3 * HD]
                both[rows, HD : 2 * HD] = grad[ds(t * CHUNK, CHUNK), :]
        keys[2 * j * CHUNK : (2 * j + 2) * CHUNK, :] = main[j][:, 0 : 2 * HD]
        keys[(8 + 2 * j) * CHUNK : (10 + 2 * j) * CHUNK, :] = other[j][...]

    def pair_chunk(t):
        return 4 * t + jnp.where(t < 4, 2 * r, 2 - 2 * r)

    def chunk(n, carry):
        x = lax.rem(head - (n // 2) % 4 + 4, 4)
        z = jnp.where(n < 8, 2 * r, 2 * (1 - r)) + core
        c = 4 * x + z
        i = jnp.where(n % 2 == 0, c, 31 - c)
        rows_k = ds(n * CHUNK, CHUNK)
        k = keys[rows_k, 0:HD]
        v = keys[rows_k, HD : 2 * HD]
        pos = lax.broadcasted_iota(jnp.int32, (CHUNK, 2 * CHUNK), 0).astype(F32) + (i * CHUNK).astype(F32)

        def step(t, totals):
            d_key, d_value = totals
            rows = ds(t * 2 * CHUNK, 2 * CHUNK)
            q = both[rows, 0:HD]
            g = both[rows, HD : 2 * HD]
            first = pair_chunk(t)
            begin = jnp.concatenate([starts[pl.ds(first, 1), :], starts[pl.ds(first + 1, 1), :]], axis=1)
            lanes = ds(first * CHUNK, 2 * CHUNK)
            halves = [
                jnp.broadcast_to(query_pos[pl.ds(2 * i + m, 1), lanes], (BROWS, 2 * CHUNK)) for m in range(2)
            ]
            allowed = (pos <= jnp.concatenate(halves, axis=0)) & (pos >= begin)
            h = dot_nt(k, q) * (0.5 * SCALE)
            dp = dot_nt(v, g)
            th = jnp.tanh(h)
            up = 1.0 + th
            probs = jnp.where(allowed, h * up, 0.0).astype(BF)
            d_scores = jnp.where(allowed, dp * (up * (1.0 + h - h * th)), 0.0).astype(BF)
            return d_key + dot(d_scores, q), d_value + dot(probs, g)

        low = i // 4
        low = jnp.where(pair_chunk(low) + 1 >= i, low, low + 1)
        last = bounds[1, i]
        high = last // (4 * CHUNK)
        high = jnp.where(pair_chunk(high) * CHUNK <= last, high, high - 1)
        zero = jnp.zeros((CHUNK, HD), F32)
        d_key, d_value = lax.fori_loop(low, high + 1, step, (zero, zero))
        sums[rows_k, 0:HD] = (d_key * (0.5 * SCALE)).astype(BF)
        sums[rows_k, HD : 2 * HD] = d_value.astype(BF)
        return carry

    lax.fori_loop(0, 16, chunk, 0)
    for j in range(4):
        out_main[j][...] = sums[2 * j * CHUNK : (2 * j + 2) * CHUNK, :]
        out_other[j][...] = sums[(8 + 2 * j) * CHUNK : (10 + 2 * j) * CHUNK, :]


def output_kernel(meta, *rest):
    parts, rest = rest[:4], rest[4:]
    pre, dmixed, hist, w_out, w_in = rest[:5]
    out, partial = rest[5:7]
    attn = rest[7]
    for j in range(4):
        attn[:, ds(lax.rem(meta[0] + j, 4) * HD, HD)] = parts[j][...].astype(F32)
    hat, _ = row_statistics(attn[...])
    u_pre = pre[:, 0:WIDTH]
    u = silu(u_pre).astype(BF).astype(F32)
    mixed = (hat * u).astype(BF)
    out[...] = (hist[...].astype(F32) + dot(mixed, w_out[...])).astype(BF)
    d_pre = (dmixed[...] * hat * silu_slope(u_pre)).astype(BF)
    partial[...] = dot_nt(d_pre, w_in[:, 0:WIDTH])


def input_grad_kernel(meta, dest, slot, *rest):
    queries, main, other = (rest[4 * n : 4 * n + 4] for n in range(3))
    pre, partial, hist, incoming, w_in = rest[12:17]
    outs = rest[17:25]
    d_act, result = rest[25:27]
    for j in range(4):
        head = lax.rem(meta[0] + j, 4) * HD
        both = main[j][...].astype(F32) + other[j][...].astype(F32)
        d_act[:, ds(head, HD)] = both[:, HD : 2 * HD]
        d_act[:, ds(WIDTH + head, HD)] = queries[j][...].astype(F32)
        d_act[:, ds(2 * WIDTH + head, HD)] = both[:, 0:HD]
    total = partial[...]
    for n in range(3):
        cols = slice((n + 1) * WIDTH, (n + 2) * WIDTH)
        d_pre = (d_act[:, n * WIDTH : (n + 1) * WIDTH] * silu_slope(pre[:, cols])).astype(BF)
        total = total + dot_nt(d_pre, w_in[:, cols])
    hat, inverse = row_statistics(hist[...].astype(F32))
    result[...] = (incoming[...].astype(F32) + norm_backward(total, hat, inverse)).astype(BF)
    own = meta[2] * 2 + meta[3]
    for k in range(8):
        outs[k][...] = jnp.zeros_like(outs[k])
        source = lax.rem(own - k + 8, 8)
        for p in range(NBLK):

            @pl.when(dest[source * NBLK + p] == own)
            def _():
                outs[k][...] = result[ds(slot[source * NBLK + p] * BROWS, BROWS), :]


def table_grad_kernel(meta, dest, ids, *rest):
    blocks, out, rows = rest[:8], rest[8], rest[9]
    step = pl.program_id(0)
    tile = out.shape[2]

    @pl.when(step == 0)
    def _():
        own = meta[2] * 2 + meta[3]
        for k in range(8):
            for p in range(NBLK):

                @pl.when(dest[own * NBLK + p] == lax.rem(own + k, 8))
                def _():
                    rows[p * BROWS : (p + 1) * BROWS, :] = blocks[k][...]

    number = lax.broadcasted_iota(jnp.int32, (tile, ROWS), 0) + step * tile
    hits = jnp.where(number == ids[...], 1.0, 0.0).astype(BF)
    out[0, 0] = dot(hits, rows[...]).astype(BF)


def body(table, row_ids, dests, slots, lengths, tile_mask, w_in, w_out, output_gradient):
    x, z, y, c = (lax.axis_index(a).astype(jnp.int32) for a in AXES)
    dest = dests.reshape(8 * NBLK)
    slot = slots.reshape(8 * NBLK)
    tab_rows = table.shape[2]

    place_info = jnp.stack([x, z, y, c])
    swap = core_pairs()
    mask = tile_mask[0]
    bounds, starts, key_pos, query_pos, dmixed = call(
        prepare_kernel,
        [place_info, lengths[0], send(lengths[0], swap), mask, send(mask, swap), output_gradient[0], w_out],
        [SMEM] * 3 + [VMEM] * 4,
        [
            shape((8, CHUNK), jnp.int32),
            shape((32, CHUNK), F32),
            shape((64, LENGTH), F32),
            shape((64, LENGTH), F32),
            shape((ROWS, WIDTH), F32),
        ],
        flops=2 * ROWS * WIDTH * WIDTH,
        name="prepare",
    )

    tiles = 8
    tile = tab_rows // tiles
    block_shape = shape((BROWS, WIDTH), BF)
    whole_block = pl.BlockSpec((BROWS, WIDTH), lambda i: (0, 0))
    outgoing = pl.pallas_call(
        lookup_kernel,
        grid=(tiles,),
        in_specs=[
            SMEM,
            SMEM,
            pl.BlockSpec((2, CHUNK), lambda i: (0, 0)),
            pl.BlockSpec((1, 1, tile, WIDTH), lambda i: (0, 0, i, 0)),
        ],
        out_specs=[whole_block] * 8,
        out_shape=[block_shape] * 8,
        scratch_shapes=[pltpu.VMEM((ROWS, WIDTH), F32), pltpu.VMEM((ROWS, CHUNK), F32)],
        name="lookup",
    )(place_info, dest, row_ids.reshape(2, CHUNK), table)
    blocks = [outgoing[0]] + [send(outgoing[k], tab_pairs(k)) for k in range(1, 8)]

    incoming = output_gradient[0]
    qkv = shape((ROWS, 3 * HD), BF)
    two = shape((ROWS, 2 * HD), BF)
    one = shape((ROWS, HD), BF)
    hist, pre, *pieces = call(
        project_kernel,
        [place_info, dest, slot, *blocks, w_in, dmixed],
        [SMEM] * 3 + [VMEM] * 10,
        [shape((ROWS, WIDTH), BF), shape((ROWS, 4 * WIDTH), F32)] + [qkv] * 4 + [two] * 4 + [one] * 4,
        [pltpu.VMEM((ROWS, 4 * WIDTH), BF), pltpu.VMEM((ROWS, WIDTH), BF)],
        flops=2 * ROWS * WIDTH * 4 * WIDTH,
        name="project",
    )
    main = [send(pieces[j], main_pairs(j)) for j in range(4)]
    other = [send(pieces[4 + j], other_pairs(j)) for j in range(4)]
    extra = [send(pieces[8 + j], main_pairs(j)) for j in range(4)]
    smain = [send(v, swap) for v in main]
    sother = [send(v, swap) for v in other]

    quarter = LENGTH // 4
    keys, queries, grads, attn, *returned = call(
        forward_kernel,
        [place_info, bounds, starts, key_pos, *main, *other, *smain, *sother, *extra],
        [SMEM] * 2 + [VMEM] * 22,
        [
            shape((LENGTH, 2 * HD), BF),
            shape((quarter, HD), BF),
            shape((quarter, HD), BF),
            shape((quarter, HD), F32),
        ]
        + [one] * 4
        + [shape((8, quarter), F32)],
        flops=10**9,
        name="forward",
    )
    stats = returned.pop()
    from_heads = [send(stats, head_pairs(k)) for k in range(1, 4)]
    attn_back = [send(returned[j], back(main_pairs(j))) for j in range(4)]

    (d_attn,) = call(
        attn_grad_kernel,
        [stats, *from_heads, attn, grads],
        [VMEM] * 6,
        [shape((quarter, HD), BF)],
        flops=10**7,
        name="attn_grad",
    )
    d_swap = send(d_attn, swap)
    d_query = call(
        query_grad_kernel,
        [place_info, bounds, starts, key_pos, keys, queries, d_attn],
        [SMEM] * 2 + [VMEM] * 5,
        [one] * 4,
        [pltpu.VMEM((quarter, HD), BF)],
        flops=2 * 10**9,
        name="query_grad",
    )
    query_back = [send(d_query[j], back(main_pairs(j))) for j in range(4)]
    d_keys = call(
        key_grad_kernel,
        [place_info, bounds, starts, query_pos, *main, *other, *smain, d_attn, d_swap],
        [SMEM] * 2 + [VMEM] * 16,
        [two] * 8,
        [
            pltpu.VMEM((LENGTH // 2, 2 * HD), BF),
            pltpu.VMEM((LENGTH // 2, 2 * HD), BF),
            pltpu.VMEM((LENGTH // 2, 2 * HD), BF),
        ],
        flops=3 * 10**9,
        name="key_grad",
    )
    main_back = [send(d_keys[j], back(main_pairs(j))) for j in range(4)]
    other_back = [send(d_keys[4 + j], back(other_pairs(j))) for j in range(4)]

    layer_out, partial = call(
        output_kernel,
        [place_info, *attn_back, pre, dmixed, hist, w_out, w_in],
        [SMEM] + [VMEM] * 9,
        [shape((ROWS, WIDTH), BF), shape((ROWS, WIDTH), F32)],
        [pltpu.VMEM((ROWS, WIDTH), F32)],
        flops=4 * ROWS * WIDTH * WIDTH,
        name="output",
    )
    returning = call(
        input_grad_kernel,
        [place_info, dest, slot, *query_back, *main_back, *other_back, pre, partial, hist, incoming, w_in],
        [SMEM] * 3 + [VMEM] * 17,
        [block_shape] * 8,
        [pltpu.VMEM((ROWS, 3 * WIDTH), F32), pltpu.VMEM((ROWS, WIDTH), BF)],
        flops=6 * ROWS * WIDTH * WIDTH,
        name="input_grad",
    )
    came_back = [returning[0]] + [send(returning[k], back(tab_pairs(k))) for k in range(1, 8)]
    table_grad = pl.pallas_call(
        table_grad_kernel,
        grid=(tiles,),
        in_specs=[SMEM, SMEM, pl.BlockSpec((1, ROWS), lambda i: (0, 0))] + [whole_block] * 8,
        out_specs=pl.BlockSpec((1, 1, tile, WIDTH), lambda i: (0, 0, i, 0)),
        out_shape=shape((1, 1, tab_rows, WIDTH), BF),
        scratch_shapes=[pltpu.VMEM((ROWS, WIDTH), BF)],
        name="table_grad",
    )(place_info, dest, row_ids.reshape(1, ROWS), *came_back)
    return layer_out.reshape(1, ROWS, WIDTH), table_grad


def solution(mesh):
    fine = Mesh(mesh.devices.reshape(4, 4, 4, 2), AXES)
    ctx, tab = ("x", "z"), ("y", "c")
    in_specs = (
        P(ctx, tab, None, None),
        P(ctx, tab, None),
        P(ctx, None, None),
        P(ctx, None, None),
        P(tab, None),
        P(tab, None, None),
        P(),
        P(),
        P(tab, ctx, None),
    )
    out_specs = (P(tab, ctx, None), P(ctx, tab, None, None))
    return jax.shard_map(body, mesh=fine, in_specs=in_specs, out_specs=out_specs, check_vma=False)
```

```python
import functools

import jax
import jax.numpy as jnp
from jax import lax
from jax.experimental import pallas as pl
from jax.experimental.pallas import tpu as pltpu
from jax.sharding import Mesh, PartitionSpec as P

HEADS = 4
BROWS = 64
NBLK = 4
WIDTH = 512
HD = 128
ROWS = 256
CHUNK = 128
LENGTH = 4096
EPS = 1e-05
BF = jnp.bfloat16
F32 = jnp.float32
AXES = ("x", "z", "y", "c")
FAR = 1e9
KEY_TILE = 256
SCALE = HD ** (-0.5)


def device_id(x, z, y, c):
    return ((x * 4 + z) * 4 + y) * 2 + c


def all_coords():
    return [(x, z, y, c) for x in range(4) for z in range(4) for y in range(4) for c in range(2)]


def tab_pairs(step):
    out = []
    for x, z, y, c in all_coords():
        y2, c2 = divmod((y * 2 + c + step) % 8, 2)
        out.append((device_id(x, z, y, c), device_id(x, z, y2, c2)))
    return out


def moved(axis, step):
    out = []
    for x, z, y, c in all_coords():
        to = ((x + step) % 4, z) if axis == c else (x, (z + step) % 4)
        out.append((device_id(x, z, y, c), device_id(*to, y, c)))
    return out


def head_pairs(step):
    return moved(0, step)


def row_pairs(step):
    return moved(1, step)


def back(pairs):
    return [(b, a) for a, b in pairs]


def send(value, pairs):
    return lax.ppermute(value, AXES, pairs)


def dot(a, b):
    return jnp.dot(a, b, preferred_element_type=F32)


def dot_nt(a, b):
    return lax.dot_general(a, b, (((1,), (1,)), ((), ())), preferred_element_type=F32)


def silu(z):
    h = 0.5 * z
    return h + h * jnp.tanh(h)


def silu_slope(z):
    h = 0.5 * z
    t = jnp.tanh(h)
    return 0.5 * (1.0 + t) * (1.0 + h * (1.0 - t))


def row_statistics(x):
    mean = jnp.mean(x, axis=-1, keepdims=True)
    centred = x - mean
    inverse = lax.rsqrt(jnp.mean(centred * centred, axis=-1, keepdims=True) + EPS)
    return centred * inverse, inverse


def norm_backward(grad, hat, inverse):
    first = jnp.mean(grad, axis=-1, keepdims=True)
    second = jnp.mean(grad * hat, axis=-1, keepdims=True)
    return inverse * (grad - first - hat * second)


def column_of(row):
    return jnp.transpose(jnp.broadcast_to(row, (CHUNK, CHUNK)))


def ds(start, size):
    return pl.ds(pl.multiple_of(start, size), size)


VMEM = pl.BlockSpec(memory_space=pltpu.VMEM)
SMEM = pl.BlockSpec(memory_space=pltpu.SMEM)


def shape(dims, dtype):
    return jax.ShapeDtypeStruct(dims, dtype)


def call(kernel, ins, specs, outs, scratch=(), flops=0, name=None):
    moved = sum(a.size * a.dtype.itemsize for a in ins)
    moved += sum(o.size * jnp.dtype(o.dtype).itemsize for o in outs)
    return pl.pallas_call(
        kernel,
        out_shape=outs,
        in_specs=specs,
        out_specs=[VMEM] * len(outs),
        scratch_shapes=list(scratch),
        compiler_params=pltpu.CompilerParams(vmem_limit_bytes=40 * 1024 * 1024),
        cost_estimate=pl.CostEstimate(flops=flops, bytes_accessed=moved, transcendentals=0),
        name=name,
    )(*ins)


def lookup_kernel(meta, dest, ids_ref, table_ref, *rest):
    outs, (total, column) = rest[:8], rest[8:]
    step = pl.program_id(0)
    tile = table_ref.shape[2]

    @pl.when(step == 0)
    def _():
        for k in range(8):
            outs[k][...] = jnp.zeros_like(outs[k])
        total[...] = jnp.zeros_like(total)
        for b in range(2):
            column[b * CHUNK : (b + 1) * CHUNK, :] = column_of(ids_ref[b : b + 1, :].astype(F32))

    lane = lax.broadcasted_iota(jnp.int32, (ROWS, CHUNK), 1).astype(F32)
    base = (step * tile).astype(F32)
    wanted = column[...] - base
    hits = [jnp.where(wanted == lane + float(n * CHUNK), 1.0, 0.0).astype(BF) for n in range(tile // CHUNK)]
    total[...] += dot(jnp.concatenate(hits, axis=1), table_ref[0, 0])

    @pl.when(step == pl.num_programs(0) - 1)
    def _():
        own = meta[2] * 2 + meta[3]
        for k in range(8):
            for p in range(NBLK):

                @pl.when(dest[own * NBLK + p] == lax.rem(own + k, 8))
                def _():
                    outs[k][...] = total[p * BROWS : (p + 1) * BROWS, :].astype(BF)


def prepare_kernel(lengths, tile_mask, incoming, w_out, bounds, starts, key_pos, query_pos, dmixed):
    chunk = lax.broadcasted_iota(jnp.int32, (32, CHUNK), 0)
    position = chunk * CHUNK + lax.broadcasted_iota(jnp.int32, (32, CHUNK), 1)
    lane = lax.broadcasted_iota(jnp.int32, (8, CHUNK), 1)
    row = lax.broadcasted_iota(jnp.int32, (8, CHUNK), 0)
    first, last = lane * CHUNK, lane * CHUNK + CHUNK - 1
    start = jnp.zeros((32, CHUNK), jnp.int32)
    chunk_start = jnp.zeros((8, CHUNK), jnp.int32)
    chunk_stop = jnp.full((8, CHUNK), LENGTH, jnp.int32)
    end = jnp.int32(0)
    for d in range(lengths.shape[0]):
        end = end + lengths[d]
        start = jnp.where(position >= end, end, start)
        chunk_start = jnp.where(first >= end, end, chunk_start)
        chunk_stop = jnp.where(last < end, jnp.minimum(chunk_stop, end), chunk_stop)
    starts[...] = start.astype(F32)
    bounds[...] = jnp.where(row == 0, chunk_start, chunk_stop - 1)
    mask = tile_mask[...].astype(F32)
    turned = jnp.transpose(mask).astype(BF)
    mask = mask.astype(BF)
    for n in range(8):
        cols = slice(n * WIDTH, (n + 1) * WIDTH)
        spot = lax.broadcasted_iota(jnp.int32, (BROWS, WIDTH), 1) + n * WIDTH
        pick = jnp.where(
            lax.broadcasted_iota(jnp.int32, (BROWS, WIDTH), 0) == spot // BROWS, 1.0, 0.0
        ).astype(BF)
        spot = spot.astype(F32)
        key_pos[:, cols] = jnp.where(dot(mask, pick) > 0.5, spot, FAR)
        query_pos[:, cols] = jnp.where(dot(turned, pick) > 0.5, spot, -1.0)
    dmixed[...] = dot_nt(incoming[...], w_out[...])


def project_kernel(meta, dest, slot, *rest):
    blocks, (w_ref, dmixed_ref), rest = rest[:8], rest[8:10], rest[10:]
    hist, pre = rest[:2]
    outs = rest[2:6]
    act, grads = rest[6:]
    own = meta[2] * 2 + meta[3]
    for k in range(8):
        source = lax.rem(own - k + 8, 8)
        for p in range(NBLK):

            @pl.when(dest[source * NBLK + p] == own)
            def _():
                hist[ds(slot[source * NBLK + p] * BROWS, BROWS), :] = blocks[k][...]

    hat, _ = row_statistics(hist[...].astype(F32))
    normed = hat.astype(BF)
    for n in range(4):
        cols = slice(n * WIDTH, (n + 1) * WIDTH)
        part = dot(normed, w_ref[:, cols])
        pre[:, cols] = part
        act[:, cols] = silu(part).astype(BF)
    grads[...] = (dmixed_ref[...] * act[:, 0:WIDTH].astype(F32)).astype(BF)
    for j in range(4):
        head = lax.rem(line(meta)[0] + j, 4) * HD
        outs[j][:, 0:HD] = act[:, ds(3 * WIDTH + head, HD)]
        outs[j][:, HD : 2 * HD] = act[:, ds(WIDTH + head, HD)]
        outs[j][:, 2 * HD : 3 * HD] = act[:, ds(2 * WIDTH + head, HD)]
        outs[j][:, 3 * HD : 4 * HD] = grads[:, ds(head, HD)]


def line(meta):
    first = meta[3] == 0
    return jnp.where(first, meta[0], meta[1]), jnp.where(first, meta[1], meta[0])


def chunk_of(t, row, core):
    spread = 4 * t + jnp.where(t < 4, row, 3 - row)
    solid = t + jnp.where(t < 4, 4 * row, 24 - 4 * row)
    return jnp.where(core == 0, spread, solid)


def pieces_of(meta):
    head = line(meta)[0]
    for j in range(4):
        source = lax.rem(head - j + 4, 4)
        yield j, 0, source
        yield j, CHUNK, 7 - source


def collect_kernel(meta, p0, p1, p2, p3, keys, queries, grads):
    pieces = (p0, p1, p2, p3)
    for j, low, t in pieces_of(meta):
        rows, part = ds(t * CHUNK, CHUNK), pieces[j]
        keys[rows, :] = part[low : low + CHUNK, 0 : 2 * HD]
        queries[rows, :] = part[low : low + CHUNK, 2 * HD : 3 * HD]
        grads[rows, :] = part[low : low + CHUNK, 3 * HD : 4 * HD]


def place_rows(meta, parts, out):
    row, core = line(meta)[1], meta[3]
    for k in range(4):
        other = lax.rem(row - k + 4, 4)
        for t in range(8):
            chunk = chunk_of(t, other, core)
            out[ds(chunk * CHUNK, CHUNK), :] = parts[k][t * CHUNK : (t + 1) * CHUNK, :]


def valid_keys(starts, key_pos, i, tile):
    pos = lax.broadcasted_iota(jnp.int32, (CHUNK, CHUNK), 0).astype(F32) + (i * CHUNK).astype(F32)
    start = column_of(starts[pl.ds(i, 1), :])
    repeat = KEY_TILE // CHUNK
    pos = jnp.concatenate([pos] * repeat, axis=1)
    start = jnp.concatenate([start] * repeat, axis=1)

    def at(tile):
        halves = [
            jnp.broadcast_to(key_pos[pl.ds(2 * i + n, 1), ds(tile * KEY_TILE, KEY_TILE)], (BROWS, KEY_TILE))
            for n in range(2)
        ]
        key = jnp.concatenate(halves, axis=0)
        return (key >= start) & (key <= pos)

    return at


def forward_kernel(meta, bounds, starts, key_pos, k0, k1, k2, k3, queries, grads, keys, attn, r0, r1, r2, r3, stats):
    returned = (r0, r1, r2, r3)
    row, core = line(meta)[1], meta[3]
    place_rows(meta, (k0, k1, k2, k3), keys)

    def chunk(t, carry):
        i = chunk_of(t, row, core)
        allowed = valid_keys(starts, key_pos, i, KEY_TILE)
        q = queries[ds(t * CHUNK, CHUNK), :]

        def step(n, total):
            rows = ds(n * KEY_TILE, KEY_TILE)
            h = dot_nt(q, keys[rows, 0:HD]) * (0.5 * SCALE)
            probs = jnp.where(allowed(n), h + h * jnp.tanh(h), 0.0).astype(BF)
            return total + dot(probs, keys[rows, HD : 2 * HD])

        first = bounds[0, i] // KEY_TILE
        last = (i * CHUNK + CHUNK - 1) // KEY_TILE
        total = lax.fori_loop(first, last + 1, step, jnp.zeros((CHUNK, HD), F32))
        rows = ds(t * CHUNK, CHUNK)
        attn[rows, :] = total
        e = grads[rows, :].astype(F32)
        mean = jnp.mean(total, axis=1, keepdims=True)
        centred = total - mean
        lane = lax.broadcasted_iota(jnp.int32, (CHUNK, CHUNK), 1)
        packed = jnp.where(lane == 0, mean, 0.0)
        packed = jnp.where(lane == 1, jnp.sum(centred * centred, axis=1, keepdims=True), packed)
        packed = jnp.where(lane == 2, jnp.sum(e, axis=1, keepdims=True), packed)
        packed = jnp.where(lane == 3, jnp.sum(e * centred, axis=1, keepdims=True), packed)
        stats[:, rows] = jnp.transpose(packed)[0:8, :]
        return carry

    lax.fori_loop(0, 8, chunk, 0)
    for j, low, t in pieces_of(meta):
        returned[j][low : low + CHUNK, :] = attn[ds(t * CHUNK, CHUNK), :].astype(BF)


def attn_grad_kernel(s0, s1, s2, s3, attn, grads, out):
    parts = [s[...] for s in (s0, s1, s2, s3)]
    means = [s[0:1, :] for s in parts]
    mean = (means[0] + means[1] + means[2] + means[3]) * 0.25
    spread = sum(s[1:2, :] + HD * (m - mean) * (m - mean) for s, m in zip(parts, means))
    inverse = lax.rsqrt(spread * (1.0 / WIDTH) + EPS)
    e_mean = sum(s[2:3, :] for s in parts) * (1.0 / WIDTH)
    e_on = sum(s[3:4, :] + (m - mean) * s[2:3, :] for s, m in zip(parts, means))
    e_on = e_on * inverse * (1.0 / WIDTH)
    for t in range(8):
        rows = slice(t * CHUNK, (t + 1) * CHUNK)
        cols = [column_of(v[:, rows]) for v in (mean, inverse, e_mean, e_on)]
        hat = (attn[rows, :] - cols[0]) * cols[1]
        out[rows, :] = (cols[1] * (grads[rows, :].astype(F32) - cols[2] - hat * cols[3])).astype(BF)


def query_grad_kernel(meta, bounds, starts, key_pos, keys, queries, d_attn, *rest):
    outs, total_ref = rest[:4], rest[4]
    row, core = line(meta)[1], meta[3]

    def chunk(t, carry):
        i = chunk_of(t, row, core)
        allowed = valid_keys(starts, key_pos, i, KEY_TILE)
        rows_q = ds(t * CHUNK, CHUNK)
        q = queries[rows_q, :]
        g = d_attn[rows_q, :]

        def step(n, total):
            rows = ds(n * KEY_TILE, KEY_TILE)
            k = keys[rows, 0:HD]
            h = dot_nt(q, k) * (0.5 * SCALE)
            dp = dot_nt(g, keys[rows, HD : 2 * HD])
            th = jnp.tanh(h)
            d_scores = jnp.where(allowed(n), dp * ((1.0 + th) * (1.0 + h - h * th)), 0.0)
            return total + dot(d_scores.astype(BF), k)

        first = bounds[0, i] // KEY_TILE
        last = (i * CHUNK + CHUNK - 1) // KEY_TILE
        total = lax.fori_loop(first, last + 1, step, jnp.zeros((CHUNK, HD), F32))
        total_ref[rows_q, :] = (total * (0.5 * SCALE)).astype(BF)
        return carry

    lax.fori_loop(0, 8, chunk, 0)
    for j, low, t in pieces_of(meta):
        outs[j][low : low + CHUNK, :] = total_ref[ds(t * CHUNK, CHUNK), :]


def key_grad_kernel(meta, bounds, starts, query_pos, keys, q0, q1, q2, q3, g0, g1, g2, g3, *rest):
    outs, (queries, grads, sums) = rest[:4], rest[4:]
    row, core = line(meta)[1], meta[3]
    place_rows(meta, (q0, q1, q2, q3), queries)
    place_rows(meta, (g0, g1, g2, g3), grads)
    tile = KEY_TILE

    def chunk(t, carry):
        i = chunk_of(t, row, core)
        rows_k = ds(i * CHUNK, CHUNK)
        k = keys[rows_k, 0:HD]
        v = keys[rows_k, HD : 2 * HD]
        pos = lax.broadcasted_iota(jnp.int32, (CHUNK, tile), 0).astype(F32) + (i * CHUNK).astype(F32)

        def step(n, totals):
            d_key, d_value = totals
            rows = ds(n * tile, tile)
            q = queries[rows, :]
            g = grads[rows, :]
            begin = jnp.concatenate(
                [starts[pl.ds(n * (tile // CHUNK) + m, 1), :] for m in range(tile // CHUNK)], axis=1
            )
            halves = [
                jnp.broadcast_to(query_pos[pl.ds(2 * i + m, 1), rows], (BROWS, tile)) for m in range(2)
            ]
            allowed = (pos <= jnp.concatenate(halves, axis=0)) & (pos >= begin)
            h = dot_nt(k, q) * (0.5 * SCALE)
            dp = dot_nt(v, g)
            th = jnp.tanh(h)
            up = 1.0 + th
            probs = jnp.where(allowed, h * up, 0.0).astype(BF)
            d_scores = jnp.where(allowed, dp * (up * (1.0 + h - h * th)), 0.0).astype(BF)
            return d_key + dot(d_scores, q), d_value + dot(probs, g)

        zero = jnp.zeros((CHUNK, HD), F32)
        low, high = (i * CHUNK) // tile, bounds[1, i] // tile
        d_key, d_value = lax.fori_loop(low, high + 1, step, (zero, zero))
        out = ds(t * CHUNK, CHUNK)
        sums[out, 0:HD] = (d_key * (0.5 * SCALE)).astype(BF)
        sums[out, HD : 2 * HD] = d_value.astype(BF)
        return carry

    lax.fori_loop(0, 8, chunk, 0)
    for j, low, t in pieces_of(meta):
        outs[j][low : low + CHUNK, :] = sums[ds(t * CHUNK, CHUNK), :]


def output_kernel(meta, *rest):
    parts, rest = rest[:4], rest[4:]
    pre, dmixed, hist, w_out, w_in = rest[:5]
    out, partial = rest[5:7]
    attn = rest[7]
    for j in range(4):
        attn[:, ds(lax.rem(line(meta)[0] + j, 4) * HD, HD)] = parts[j][...].astype(F32)
    hat, _ = row_statistics(attn[...])
    u_pre = pre[:, 0:WIDTH]
    u = silu(u_pre).astype(BF).astype(F32)
    mixed = (hat * u).astype(BF)
    out[...] = (hist[...].astype(F32) + dot(mixed, w_out[...])).astype(BF)
    d_pre = (dmixed[...] * hat * silu_slope(u_pre)).astype(BF)
    partial[...] = dot_nt(d_pre, w_in[:, 0:WIDTH])


def input_grad_kernel(meta, dest, slot, *rest):
    queries, both = rest[:4], rest[4:8]
    pre, partial, hist, incoming, w_in = rest[8:13]
    outs = rest[13:21]
    d_act, result = rest[21:]
    for j in range(4):
        head = lax.rem(line(meta)[0] + j, 4) * HD
        d_act[:, ds(head, HD)] = both[j][:, HD : 2 * HD].astype(F32)
        d_act[:, ds(WIDTH + head, HD)] = queries[j][...].astype(F32)
        d_act[:, ds(2 * WIDTH + head, HD)] = both[j][:, 0:HD].astype(F32)
    total = partial[...]
    for n in range(3):
        cols = slice((n + 1) * WIDTH, (n + 2) * WIDTH)
        d_pre = (d_act[:, n * WIDTH : (n + 1) * WIDTH] * silu_slope(pre[:, cols])).astype(BF)
        total = total + dot_nt(d_pre, w_in[:, cols])
    hat, inverse = row_statistics(hist[...].astype(F32))
    result[...] = (incoming[...].astype(F32) + norm_backward(total, hat, inverse)).astype(BF)
    own = meta[2] * 2 + meta[3]
    for k in range(8):
        outs[k][...] = jnp.zeros_like(outs[k])
        source = lax.rem(own - k + 8, 8)
        for p in range(NBLK):

            @pl.when(dest[source * NBLK + p] == own)
            def _():
                outs[k][...] = result[ds(slot[source * NBLK + p] * BROWS, BROWS), :]


def table_grad_kernel(meta, dest, ids, *rest):
    blocks, out, rows = rest[:8], rest[8], rest[9]
    step = pl.program_id(0)
    tile = out.shape[2]

    @pl.when(step == 0)
    def _():
        own = meta[2] * 2 + meta[3]
        for k in range(8):
            for p in range(NBLK):

                @pl.when(dest[own * NBLK + p] == lax.rem(own + k, 8))
                def _():
                    rows[p * BROWS : (p + 1) * BROWS, :] = blocks[k][...]

    number = lax.broadcasted_iota(jnp.int32, (tile, ROWS), 0) + step * tile
    hits = jnp.where(number == ids[...], 1.0, 0.0).astype(BF)
    out[0, 0] = dot(hits, rows[...]).astype(BF)


def body(table, row_ids, dests, slots, lengths, tile_mask, w_in, w_out, output_gradient):
    x, z, y, c = (lax.axis_index(a).astype(jnp.int32) for a in AXES)
    dest = dests.reshape(8 * NBLK)
    slot = slots.reshape(8 * NBLK)
    tab_rows = table.shape[2]

    place_info = jnp.stack([x, z, y, c])
    bounds, starts, key_pos, query_pos, dmixed = call(
        prepare_kernel,
        [lengths[0], tile_mask[0], output_gradient[0], w_out],
        [SMEM] + [VMEM] * 3,
        [
            shape((8, CHUNK), jnp.int32),
            shape((32, CHUNK), F32),
            shape((64, LENGTH), F32),
            shape((64, LENGTH), F32),
            shape((ROWS, WIDTH), F32),
        ],
        flops=2 * ROWS * WIDTH * WIDTH,
        name="prepare",
    )

    tiles = 8
    tile = tab_rows // tiles
    block_shape = shape((BROWS, WIDTH), BF)
    whole_block = pl.BlockSpec((BROWS, WIDTH), lambda i: (0, 0))
    outgoing = pl.pallas_call(
        lookup_kernel,
        grid=(tiles,),
        in_specs=[
            SMEM,
            SMEM,
            pl.BlockSpec((2, CHUNK), lambda i: (0, 0)),
            pl.BlockSpec((1, 1, tile, WIDTH), lambda i: (0, 0, i, 0)),
        ],
        out_specs=[whole_block] * 8,
        out_shape=[block_shape] * 8,
        scratch_shapes=[pltpu.VMEM((ROWS, WIDTH), F32), pltpu.VMEM((ROWS, CHUNK), F32)],
        name="lookup",
    )(place_info, dest, row_ids.reshape(2, CHUNK), table)
    blocks = [outgoing[0]] + [send(outgoing[k], tab_pairs(k)) for k in range(1, 8)]

    four = shape((ROWS, 4 * HD), BF)
    two = shape((ROWS, 2 * HD), BF)
    one = shape((ROWS, HD), BF)
    quarter = LENGTH // 4
    rows_two = shape((quarter, 2 * HD), BF)
    rows_one = shape((quarter, HD), BF)

    def to_heads(values):
        return [values[0]] + [send(values[j], head_pairs(j)) for j in range(1, 4)]

    def to_owners(values):
        return [values[0]] + [send(values[j], back(head_pairs(j))) for j in range(1, 4)]

    def over_rows(value):
        return [value] + [send(value, row_pairs(k)) for k in range(1, 4)]

    hist, pre, *pieces = call(
        project_kernel,
        [place_info, dest, slot, *blocks, w_in, dmixed],
        [SMEM] * 3 + [VMEM] * 10,
        [shape((ROWS, WIDTH), BF), shape((ROWS, 4 * WIDTH), F32)] + [four] * 4,
        [pltpu.VMEM((ROWS, 4 * WIDTH), BF), pltpu.VMEM((ROWS, WIDTH), BF)],
        flops=2 * ROWS * WIDTH * 4 * WIDTH,
        name="project",
    )
    own_keys, queries, grads = call(
        collect_kernel,
        [place_info, *to_heads(pieces)],
        [SMEM] + [VMEM] * 4,
        [rows_two, rows_one, rows_one],
        name="collect",
    )
    keys, attn, *returned = call(
        forward_kernel,
        [place_info, bounds, starts, key_pos, *over_rows(own_keys), queries, grads],
        [SMEM] * 2 + [VMEM] * 8,
        [shape((LENGTH, 2 * HD), BF), shape((quarter, HD), F32)] + [one] * 4 + [shape((8, quarter), F32)],
        flops=10**9,
        name="forward",
    )
    stats = returned.pop()
    from_heads = to_heads([stats] * 4)
    attn_back = to_owners(returned)
    (d_attn,) = call(
        attn_grad_kernel,
        [*from_heads, attn, grads],
        [VMEM] * 6,
        [rows_one],
        flops=10**7,
        name="attn_grad",
    )
    d_query = call(
        query_grad_kernel,
        [place_info, bounds, starts, key_pos, keys, queries, d_attn],
        [SMEM] * 2 + [VMEM] * 5,
        [one] * 4,
        [pltpu.VMEM((quarter, HD), BF)],
        flops=2 * 10**9,
        name="query_grad",
    )
    query_back = to_owners(d_query)
    d_keys = call(
        key_grad_kernel,
        [place_info, bounds, starts, query_pos, keys, *over_rows(queries), *over_rows(d_attn)],
        [SMEM] * 2 + [VMEM] * 11,
        [two] * 4,
        [pltpu.VMEM((LENGTH, HD), BF), pltpu.VMEM((LENGTH, HD), BF), pltpu.VMEM((quarter, 2 * HD), BF)],
        flops=3 * 10**9,
        name="key_grad",
    )
    keys_back = to_owners(d_keys)

    layer_out, partial = call(
        output_kernel,
        [place_info, *attn_back, pre, dmixed, hist, w_out, w_in],
        [SMEM] + [VMEM] * 9,
        [shape((ROWS, WIDTH), BF), shape((ROWS, WIDTH), F32)],
        [pltpu.VMEM((ROWS, WIDTH), F32)],
        flops=4 * ROWS * WIDTH * WIDTH,
        name="output",
    )
    returning = call(
        input_grad_kernel,
        [place_info, dest, slot, *query_back, *keys_back, pre, partial, hist, output_gradient[0], w_in],
        [SMEM] * 3 + [VMEM] * 13,
        [block_shape] * 8,
        [pltpu.VMEM((ROWS, 3 * WIDTH), F32), pltpu.VMEM((ROWS, WIDTH), BF)],
        flops=6 * ROWS * WIDTH * WIDTH,
        name="input_grad",
    )
    came_back = [returning[0]] + [send(returning[k], back(tab_pairs(k))) for k in range(1, 8)]
    table_grad = pl.pallas_call(
        table_grad_kernel,
        grid=(tiles,),
        in_specs=[SMEM, SMEM, pl.BlockSpec((1, ROWS), lambda i: (0, 0))] + [whole_block] * 8,
        out_specs=pl.BlockSpec((1, 1, tile, WIDTH), lambda i: (0, 0, i, 0)),
        out_shape=shape((1, 1, tab_rows, WIDTH), BF),
        scratch_shapes=[pltpu.VMEM((ROWS, WIDTH), BF)],
        name="table_grad",
    )(place_info, dest, row_ids.reshape(1, ROWS), *came_back)
    return layer_out.reshape(1, ROWS, WIDTH), table_grad


def solution(mesh):
    fine = Mesh(mesh.devices.reshape(4, 4, 4, 2), AXES)
    ctx, tab = ("x", "z"), ("y", "c")
    in_specs = (
        P(ctx, tab, None, None),
        P(ctx, tab, None),
        P(ctx, None, None),
        P(ctx, None, None),
        P(tab, None),
        P(tab, None, None),
        P(),
        P(),
        P(tab, ctx, None),
    )
    out_specs = (P(tab, ctx, None), P(ctx, tab, None, None))
    return jax.shard_map(body, mesh=fine, in_specs=in_specs, out_specs=out_specs, check_vma=False)
```

```python
import functools

import jax
import jax.numpy as jnp
from jax import lax
from jax.experimental import pallas as pl
from jax.experimental.pallas import tpu as pltpu
from jax.sharding import Mesh, PartitionSpec as P

HEADS = 4
BROWS = 64
NBLK = 4
WIDTH = 512
HD = 128
ROWS = 256
CHUNK = 128
LENGTH = 4096
EPS = 1e-05
BF = jnp.bfloat16
F32 = jnp.float32
AXES = ("x", "z", "y", "c")
FAR = 1e9
KEY_TILE = 256
GROUP = 4
KEY_GROUP = 3
SCALE = HD ** (-0.5)


def device_id(x, z, y, c):
    return ((x * 4 + z) * 4 + y) * 2 + c


def all_coords():
    return [(x, z, y, c) for x in range(4) for z in range(4) for y in range(4) for c in range(2)]


def tab_pairs(step):
    out = []
    for x, z, y, c in all_coords():
        y2, c2 = divmod((y * 2 + c + step) % 8, 2)
        out.append((device_id(x, z, y, c), device_id(x, z, y2, c2)))
    return out


def moved(axis, step):
    out = []
    for x, z, y, c in all_coords():
        to = ((x + step) % 4, z) if axis == c else (x, (z + step) % 4)
        out.append((device_id(x, z, y, c), device_id(*to, y, c)))
    return out


def head_pairs(step):
    return moved(0, step)


def row_pairs(step):
    return moved(1, step)


def back(pairs):
    return [(b, a) for a, b in pairs]


def send(value, pairs):
    return lax.ppermute(value, AXES, pairs)


def dot(a, b):
    return jnp.dot(a, b, preferred_element_type=F32)


def dot_nt(a, b):
    return lax.dot_general(a, b, (((1,), (1,)), ((), ())), preferred_element_type=F32)


def silu(z):
    h = 0.5 * z
    return h + h * jnp.tanh(h)


def silu_slope(z):
    h = 0.5 * z
    t = jnp.tanh(h)
    return 0.5 * (1.0 + t) * (1.0 + h * (1.0 - t))


def row_statistics(x):
    mean = jnp.mean(x, axis=-1, keepdims=True)
    centred = x - mean
    inverse = lax.rsqrt(jnp.mean(centred * centred, axis=-1, keepdims=True) + EPS)
    return centred * inverse, inverse


def norm_backward(grad, hat, inverse):
    first = jnp.mean(grad, axis=-1, keepdims=True)
    second = jnp.mean(grad * hat, axis=-1, keepdims=True)
    return inverse * (grad - first - hat * second)


def column_of(row):
    return jnp.transpose(jnp.broadcast_to(row, (CHUNK, CHUNK)))


def ds(start, size):
    return pl.ds(pl.multiple_of(start, size), size)


VMEM = pl.BlockSpec(memory_space=pltpu.VMEM)
SMEM = pl.BlockSpec(memory_space=pltpu.SMEM)


def shape(dims, dtype):
    return jax.ShapeDtypeStruct(dims, dtype)


def call(kernel, ins, specs, outs, scratch=(), flops=0, name=None, out_specs=None, limit=40):
    moved = sum(a.size * a.dtype.itemsize for a in ins)
    moved += sum(o.size * jnp.dtype(o.dtype).itemsize for o in outs)
    return pl.pallas_call(
        kernel,
        out_shape=outs,
        in_specs=specs,
        out_specs=out_specs or [VMEM] * len(outs),
        scratch_shapes=list(scratch),
        compiler_params=pltpu.CompilerParams(vmem_limit_bytes=limit * 1024 * 1024),
        cost_estimate=pl.CostEstimate(flops=flops, bytes_accessed=moved, transcendentals=0),
        name=name,
    )(*ins)


def lookup_kernel(meta, dest, ids_ref, table, *rest):
    outs, (buffer, total, column, arrived) = rest[:8], rest[8:]
    tile = buffer.shape[1]
    copies = [
        pltpu.make_async_copy(table.at[0, 0, pl.ds(n * tile, tile), :], buffer.at[n], arrived.at[n])
        for n in range(buffer.shape[0])
    ]
    for copy in copies:
        copy.start()
    for b in range(2):
        column[b * CHUNK : (b + 1) * CHUNK, :] = column_of(ids_ref[b : b + 1, :].astype(F32))
    lane = lax.broadcasted_iota(jnp.int32, (ROWS, CHUNK), 1).astype(F32)
    for n, copy in enumerate(copies):
        hits = [
            jnp.where(column[...] == lane + float(n * tile + m * CHUNK), 1.0, 0.0).astype(BF)
            for m in range(tile // CHUNK)
        ]
        copy.wait()
        part = dot(jnp.concatenate(hits, axis=1), buffer[n])
        if n == 0:
            total[...] = part
        else:
            total[...] += part
    own = meta[2] * 2 + meta[3]
    for k in range(8):
        outs[k][...] = jnp.zeros_like(outs[k])
        for p in range(NBLK):

            @pl.when(dest[p, own] == lax.rem(own + k, 8))
            def _():
                outs[k][...] = total[p * BROWS : (p + 1) * BROWS, :].astype(BF)


def prepare_kernel(meta, lengths, tile_mask, incoming, w_out, bounds, starts, begins, key_pos, query_pos, dmixed, turned):
    row, core = line(meta)[1], meta[3]
    lane = lax.broadcasted_iota(jnp.int32, (8, CHUNK), 1)
    first, last = lane * CHUNK, lane * CHUNK + CHUNK - 1
    ends, end = [], jnp.int32(0)
    for d in range(lengths.shape[0]):
        end = end + lengths[d]
        ends.append(end)
    chunk_start = jnp.zeros((8, CHUNK), jnp.int32)
    chunk_stop = jnp.full((8, CHUNK), LENGTH, jnp.int32)
    for end in ends:
        chunk_start = jnp.where(first >= end, end, chunk_start)
        chunk_stop = jnp.where(last < end, jnp.minimum(chunk_stop, end), chunk_stop)
    row_id = lax.broadcasted_iota(jnp.int32, (8, CHUNK), 0)
    bounds[...] = jnp.where(row_id == 0, chunk_start, chunk_stop - 1)
    turned[...] = jnp.transpose(tile_mask[...].astype(F32))
    on_keys, on_queries = [], []
    for t in range(8):
        i = chunk_of(t, row, core)
        position = lax.broadcasted_iota(jnp.int32, (CHUNK, CHUNK), 0) + i * CHUNK
        begin = jnp.zeros((CHUNK, CHUNK), jnp.int32)
        for end in ends:
            begin = jnp.where(position >= end, end, begin)
        begins[t * CHUNK : (t + 1) * CHUNK, :] = begin.astype(F32)
        for m in range(2):
            on_keys.append(tile_mask[pl.ds(2 * i + m, 1), :])
            on_queries.append(turned[pl.ds(2 * i + m, 1), :])
    on_keys = jnp.concatenate(on_keys, axis=0).astype(F32).astype(BF)
    on_queries = jnp.concatenate(on_queries, axis=0).astype(BF)
    for n in range(8):
        cols = slice(n * WIDTH, (n + 1) * WIDTH)
        spot = lax.broadcasted_iota(jnp.int32, (BROWS, WIDTH), 1) + n * WIDTH
        pick = jnp.where(
            lax.broadcasted_iota(jnp.int32, (BROWS, WIDTH), 0) == spot // BROWS, 1.0, 0.0
        ).astype(BF)
        spot = spot[0:16, :]
        place = spot.astype(F32)
        key_pos[:, cols] = jnp.where(dot(on_keys, pick) > 0.5, place, FAR)
        query_pos[:, cols] = jnp.where(dot(on_queries, pick) > 0.5, place, -1.0)
        spot = spot[0:8, :]
        begin = jnp.zeros((8, WIDTH), jnp.int32)
        for end in ends:
            begin = jnp.where(spot >= end, end, begin)
        starts[:, cols] = begin.astype(F32)
    dmixed[...] = dot_nt(incoming[...], w_out[...])


def project_kernel(meta, dest, slot, *rest):
    blocks, (w_ref, dmixed_ref), rest = rest[:8], rest[8:10], rest[10:]
    hist, pre = rest[:2]
    outs = rest[2:6]
    act, grads = rest[6:]
    own = meta[2] * 2 + meta[3]
    for k in range(8):
        source = lax.rem(own - k + 8, 8)
        for p in range(NBLK):

            @pl.when(dest[p, source] == own)
            def _():
                hist[ds(slot[p, source] * BROWS, BROWS), :] = blocks[k][...]

    hat, _ = row_statistics(hist[...].astype(F32))
    normed = hat.astype(BF)
    for n in range(4):
        cols = slice(n * WIDTH, (n + 1) * WIDTH)
        part = dot(normed, w_ref[:, cols])
        pre[:, cols] = part
        act[:, cols] = silu(part).astype(BF)
    grads[...] = (dmixed_ref[...] * act[:, 0:WIDTH].astype(F32)).astype(BF)
    for j in range(4):
        head = lax.rem(line(meta)[0] + j, 4) * HD
        outs[j][:, 0:HD] = act[:, ds(3 * WIDTH + head, HD)]
        outs[j][:, HD : 2 * HD] = act[:, ds(WIDTH + head, HD)]
        outs[j][:, 2 * HD : 3 * HD] = act[:, ds(2 * WIDTH + head, HD)]
        outs[j][:, 3 * HD : 4 * HD] = grads[:, ds(head, HD)]


def line(meta):
    first = meta[3] == 0
    return jnp.where(first, meta[0], meta[1]), jnp.where(first, meta[1], meta[0])


def chunk_of(t, row, core):
    spread = 4 * t + jnp.where(t < 4, row, 3 - row)
    solid = t + jnp.where(t < 4, 4 * row, 24 - 4 * row)
    return jnp.where(core == 0, spread, solid)


def pieces_of(meta):
    head = line(meta)[0]
    for j in range(4):
        source = lax.rem(head - j + 4, 4)
        yield j, 0, source
        yield j, CHUNK, 7 - source


def collect_kernel(meta, p0, p1, p2, p3, keys, queries, grads):
    pieces = (p0, p1, p2, p3)
    for j, low, t in pieces_of(meta):
        rows, part = ds(t * CHUNK, CHUNK), pieces[j]
        keys[rows, :] = part[low : low + CHUNK, 0 : 2 * HD]
        queries[rows, :] = part[low : low + CHUNK, 2 * HD : 3 * HD]
        grads[rows, :] = part[low : low + CHUNK, 3 * HD : 4 * HD]


def place_rows(meta, parts, out):
    row, core = line(meta)[1], meta[3]
    for k in range(4):
        other = lax.rem(row - k + 4, 4)
        for t in range(8):
            chunk = chunk_of(t, other, core)
            out[ds(chunk * CHUNK, CHUNK), :] = parts[k][t * CHUNK : (t + 1) * CHUNK, :]


def list_work(pairs, tiles, span, size):
    def one_pair(p, count):
        def one(n, count):
            pairs[count] = p
            tiles[count] = n
            return count + 1

        low, high = span(2 * p)
        low_next, high_next = span(2 * p + 1)
        count = lax.fori_loop(low, high + 1, one, count)
        return lax.fori_loop(jnp.maximum(low_next, high + 1), high_next + 1, one, count)

    count = lax.fori_loop(0, 4, one_pair, jnp.int32(0))
    for u in range(size - 1):
        pairs[count + u] = 4
        tiles[count + u] = 0
    return (count + size - 1) // size


def work_scratch():
    return [pltpu.SMEM((160,), jnp.int32), pltpu.SMEM((160,), jnp.int32)]


def pair_positions(meta, p, width):
    row, core = line(meta)[1], meta[3]
    local = lax.broadcasted_iota(jnp.int32, (CHUNK, width), 0).astype(F32)
    return jnp.concatenate(
        [local + (chunk_of(2 * p + m, row, core) * CHUNK).astype(F32) for m in range(2)], axis=0
    )


def spread_rows(table, p, cols):
    return jnp.concatenate(
        [jnp.broadcast_to(table[pl.ds(4 * p + m, 1), cols], (BROWS, KEY_TILE)) for m in range(4)], axis=0
    )


def allowed_keys(meta, begins, key_pos, p, n):
    repeat = KEY_TILE // CHUNK
    pos = jnp.concatenate([pair_positions(meta, p, CHUNK)] * repeat, axis=1)
    start = jnp.concatenate([begins[ds(p * ROWS, ROWS), :]] * repeat, axis=1)
    key = spread_rows(key_pos, p, ds(n * KEY_TILE, KEY_TILE))
    return (key >= start) & (key <= pos)


def key_span(meta, bounds):
    row, core = line(meta)[1], meta[3]

    def span(t):
        i = chunk_of(t, row, core)
        return bounds[0, i] // KEY_TILE, (i * CHUNK + CHUNK - 1) // KEY_TILE

    return span


def forward_kernel(
    meta, bounds, begins, key_pos, k0, k1, k2, k3, queries, grads,
    keys, attn, passed, stats, total, pairs, tiles,
):
    passed[...] = queries[...]
    place_rows(meta, (k0, k1, k2, k3), keys)
    total[...] = jnp.zeros_like(total)
    groups = list_work(pairs, tiles, key_span(meta, bounds), GROUP)

    def group(b, carry):
        parts = []
        for u in range(GROUP):
            slot, n = pairs[b * GROUP + u], tiles[b * GROUP + u]
            p = jnp.minimum(slot, 3)
            rows = ds(n * KEY_TILE, KEY_TILE)
            h = dot_nt(queries[ds(p * ROWS, ROWS), :], keys[rows, 0:HD]) * (0.5 * SCALE)
            allowed = allowed_keys(meta, begins, key_pos, p, n)
            probs = jnp.where(allowed, h + h * jnp.tanh(h), 0.0).astype(BF)
            parts.append((slot, dot(probs, keys[rows, HD : 2 * HD])))
        for slot, part in parts:
            total[ds(slot * ROWS, ROWS), :] += part
        return carry

    lax.fori_loop(0, groups, group, 0)
    lane = lax.broadcasted_iota(jnp.int32, (CHUNK, CHUNK), 1)
    for t in range(8):
        rows = slice(t * CHUNK, (t + 1) * CHUNK)
        x = total[rows, :]
        attn[rows, :] = x
        e = grads[rows, :].astype(F32)
        mean = jnp.mean(x, axis=1, keepdims=True)
        centred = x - mean
        packed = jnp.where(lane == 0, mean, 0.0)
        packed = jnp.where(lane == 1, jnp.sum(centred * centred, axis=1, keepdims=True), packed)
        packed = jnp.where(lane == 2, jnp.sum(e, axis=1, keepdims=True), packed)
        packed = jnp.where(lane == 3, jnp.sum(e * centred, axis=1, keepdims=True), packed)
        stats[:, rows] = jnp.transpose(packed)[0:8, :]


def attn_grad_kernel(s0, s1, s2, s3, attn, grads, q1, q2, q3, out):
    parts = [s[...] for s in (s0, s1, s2, s3)]
    means = [s[0:1, :] for s in parts]
    mean = (means[0] + means[1] + means[2] + means[3]) * 0.25
    spread = sum(s[1:2, :] + HD * (m - mean) * (m - mean) for s, m in zip(parts, means))
    inverse = lax.rsqrt(spread * (1.0 / WIDTH) + EPS)
    e_mean = sum(s[2:3, :] for s in parts) * (1.0 / WIDTH)
    e_on = sum(s[3:4, :] + (m - mean) * s[2:3, :] for s, m in zip(parts, means))
    e_on = e_on * inverse * (1.0 / WIDTH)
    for t in range(8):
        rows = slice(t * CHUNK, (t + 1) * CHUNK)
        cols = [column_of(v[:, rows]) for v in (mean, inverse, e_mean, e_on)]
        hat = (attn[rows, :] - cols[0]) * cols[1]
        out[rows, :] = (cols[1] * (grads[rows, :].astype(F32) - cols[2] - hat * cols[3])).astype(BF)


def query_grad_kernel(
    meta, bounds, begins, key_pos, keys, queries, d_attn, out, total, pairs, tiles
):
    total[...] = jnp.zeros_like(total)
    groups = list_work(pairs, tiles, key_span(meta, bounds), GROUP)

    def group(b, carry):
        parts = []
        for u in range(GROUP):
            slot, n = pairs[b * GROUP + u], tiles[b * GROUP + u]
            p = jnp.minimum(slot, 3)
            rows = ds(n * KEY_TILE, KEY_TILE)
            rows_q = ds(p * ROWS, ROWS)
            k = keys[rows, 0:HD]
            h = dot_nt(queries[rows_q, :], k) * (0.5 * SCALE)
            dp = dot_nt(d_attn[rows_q, :], keys[rows, HD : 2 * HD])
            th = jnp.tanh(h)
            allowed = allowed_keys(meta, begins, key_pos, p, n)
            d_scores = jnp.where(allowed, dp * ((1.0 + th) * (1.0 + h - h * th)), 0.0)
            parts.append((slot, dot(d_scores.astype(BF), k)))
        for slot, part in parts:
            total[ds(slot * ROWS, ROWS), :] += part
        return carry

    lax.fori_loop(0, groups, group, 0)
    out[...] = (total[0 : LENGTH // 4, :] * (0.5 * SCALE)).astype(BF)


def key_grad_kernel(
    meta, bounds, starts, query_pos, keys, q0, q1, q2, q3, g0, g1, g2, g3, d_query, attn,
    r0, r1, r2, r3, queries, grads, total, pairs, tiles,
):
    outs = (r0, r1, r2, r3)
    row, core = line(meta)[1], meta[3]
    place_rows(meta, (q0, q1, q2, q3), queries)
    place_rows(meta, (g0, g1, g2, g3), grads)
    total[...] = jnp.zeros_like(total)

    def span(t):
        i = chunk_of(t, row, core)
        return (i * CHUNK) // KEY_TILE, bounds[1, i] // KEY_TILE

    groups = list_work(pairs, tiles, span, KEY_GROUP)

    def group(b, carry):
        parts = []
        for u in range(KEY_GROUP):
            slot, n = pairs[b * KEY_GROUP + u], tiles[b * KEY_GROUP + u]
            p = jnp.minimum(slot, 3)
            rows_k = ds(p * ROWS, ROWS)
            rows = ds(n * KEY_TILE, KEY_TILE)
            q, g = queries[rows, :], grads[rows, :]
            pos = pair_positions(meta, p, KEY_TILE)
            begin = jnp.broadcast_to(starts[0:1, rows], (ROWS, KEY_TILE))
            allowed = (pos <= spread_rows(query_pos, p, rows)) & (pos >= begin)
            h = dot_nt(keys[rows_k, 0:HD], q) * (0.5 * SCALE)
            dp = dot_nt(keys[rows_k, HD : 2 * HD], g)
            th = jnp.tanh(h)
            up = 1.0 + th
            probs = jnp.where(allowed, h * up, 0.0).astype(BF)
            d_scores = jnp.where(allowed, dp * (up * (1.0 + h - h * th)), 0.0).astype(BF)
            parts.append((slot, dot(d_scores, q), dot(probs, g)))
        for slot, d_key, d_value in parts:
            rows = ds(slot * ROWS, ROWS)
            total[rows, 0:HD] += d_key
            total[rows, HD : 2 * HD] += d_value
        return carry

    lax.fori_loop(0, groups, group, 0)
    for j, low, t in pieces_of(meta):
        rows = ds(t * CHUNK, CHUNK)
        outs[j][low : low + CHUNK, 0:HD] = (total[rows, 0:HD] * (0.5 * SCALE)).astype(BF)
        outs[j][low : low + CHUNK, HD : 2 * HD] = total[rows, HD : 2 * HD].astype(BF)
        outs[j][low : low + CHUNK, 2 * HD : 3 * HD] = d_query[rows, :]
        outs[j][low : low + CHUNK, 3 * HD : 4 * HD] = attn[rows, :].astype(BF)


def input_grad_kernel(meta, dest, slot, p0, p1, p2, p3, pre, dmixed, hist, incoming, w_in, *rest):
    outs, (mixed, attn, d_act, result) = rest[:8], rest[8:]
    for j, part in enumerate((p0, p1, p2, p3)):
        head = lax.rem(line(meta)[0] + j, 4) * HD
        d_act[:, ds(2 * WIDTH + head, HD)] = part[:, 0:HD].astype(F32)
        d_act[:, ds(head, HD)] = part[:, HD : 2 * HD].astype(F32)
        d_act[:, ds(WIDTH + head, HD)] = part[:, 2 * HD : 3 * HD].astype(F32)
        attn[:, ds(head, HD)] = part[:, 3 * HD : 4 * HD].astype(F32)
    on, _ = row_statistics(attn[...])
    u_pre = pre[:, 0:WIDTH]
    mixed[...] = (on * silu(u_pre).astype(BF).astype(F32)).astype(BF)
    total = dot_nt((dmixed[...] * on * silu_slope(u_pre)).astype(BF), w_in[:, 0:WIDTH])
    for n in range(3):
        cols = slice((n + 1) * WIDTH, (n + 2) * WIDTH)
        d_pre = (d_act[:, n * WIDTH : (n + 1) * WIDTH] * silu_slope(pre[:, cols])).astype(BF)
        total = total + dot_nt(d_pre, w_in[:, cols])
    hat, inverse = row_statistics(hist[...].astype(F32))
    result[...] = (incoming[...].astype(F32) + norm_backward(total, hat, inverse)).astype(BF)
    own = meta[2] * 2 + meta[3]
    for k in range(8):
        outs[k][...] = jnp.zeros_like(outs[k])
        source = lax.rem(own - k + 8, 8)
        for p in range(NBLK):

            @pl.when(dest[p, source] == own)
            def _():
                outs[k][...] = result[ds(slot[p, source] * BROWS, BROWS), :]


def output_kernel(mixed, hist, w_out, out):
    out[...] = (hist[...].astype(F32) + dot(mixed[...], w_out[...])).astype(BF)


def table_grad_kernel(meta, dest, ids, *rest):
    blocks, out, rows, buffer, sent = rest[:8], rest[8], rest[9], rest[10], rest[11]
    tile = buffer.shape[1]
    own = meta[2] * 2 + meta[3]
    for k in range(8):
        for p in range(NBLK):

            @pl.when(dest[p, own] == lax.rem(own + k, 8))
            def _():
                rows[p * BROWS : (p + 1) * BROWS, :] = blocks[k][...]

    number = lax.broadcasted_iota(jnp.int32, (tile, ROWS), 0)
    copies = []
    for n in range(buffer.shape[0]):
        hits = jnp.where(number + n * tile == ids[...], 1.0, 0.0).astype(BF)
        buffer[n] = dot(hits, rows[...]).astype(BF)
        copy = pltpu.make_async_copy(buffer.at[n], out.at[0, 0, pl.ds(n * tile, tile), :], sent.at[n])
        copy.start()
        copies.append(copy)
    for copy in copies:
        copy.wait()


def body(table, row_ids, dests, slots, lengths, tile_mask, w_in, w_out, output_gradient):
    x, z, y, c = (lax.axis_index(a).astype(jnp.int32) for a in AXES)
    dest = dests[0].T
    slot = slots[0].T
    tab_rows = table.shape[2]

    place_info = jnp.stack([x, z, y, c])
    bounds, starts, begins, key_pos, query_pos, dmixed = call(
        prepare_kernel,
        [place_info, lengths[0], tile_mask[0], output_gradient[0], w_out],
        [SMEM] * 2 + [VMEM] * 3,
        [
            shape((8, CHUNK), jnp.int32),
            shape((8, LENGTH), F32),
            shape((LENGTH // 4, CHUNK), F32),
            shape((16, LENGTH), F32),
            shape((16, LENGTH), F32),
            shape((ROWS, WIDTH), F32),
        ],
        [pltpu.VMEM((64, 64), F32)],
        flops=2 * ROWS * WIDTH * WIDTH,
        name="prepare",
    )

    tiles = 8
    tile = tab_rows // tiles
    block_shape = shape((BROWS, WIDTH), BF)
    outgoing = call(
        lookup_kernel,
        [place_info, dest, row_ids.reshape(2, CHUNK), table],
        [SMEM, SMEM, VMEM, pl.BlockSpec(memory_space=pltpu.HBM)],
        [block_shape] * 8,
        [
            pltpu.VMEM((tiles, tile, WIDTH), BF),
            pltpu.VMEM((ROWS, WIDTH), F32),
            pltpu.VMEM((ROWS, CHUNK), F32),
            pltpu.SemaphoreType.DMA((tiles,)),
        ],
        flops=2 * ROWS * tab_rows * WIDTH,
        name="lookup",
        limit=60,
    )
    blocks = [outgoing[0]] + [send(outgoing[k], tab_pairs(k)) for k in range(1, 8)]

    four = shape((ROWS, 4 * HD), BF)
    two = shape((ROWS, 2 * HD), BF)
    one = shape((ROWS, HD), BF)
    quarter = LENGTH // 4
    rows_two = shape((quarter, 2 * HD), BF)
    rows_one = shape((quarter, HD), BF)

    def to_heads(values):
        return [values[0]] + [send(values[j], head_pairs(j)) for j in range(1, 4)]

    def to_owners(values):
        return [values[0]] + [send(values[j], back(head_pairs(j))) for j in range(1, 4)]

    def over_rows(value):
        return [value] + [send(value, row_pairs(k)) for k in range(1, 4)]

    hist, pre, *pieces = call(
        project_kernel,
        [place_info, dest, slot, *blocks, w_in, dmixed],
        [SMEM] * 3 + [VMEM] * 10,
        [shape((ROWS, WIDTH), BF), shape((ROWS, 4 * WIDTH), F32)] + [four] * 4,
        [pltpu.VMEM((ROWS, 4 * WIDTH), BF), pltpu.VMEM((ROWS, WIDTH), BF)],
        flops=2 * ROWS * WIDTH * 4 * WIDTH,
        name="project",
    )
    own_keys, queries, grads = call(
        collect_kernel,
        [place_info, *to_heads(pieces)],
        [SMEM] + [VMEM] * 4,
        [rows_two, rows_one, rows_one],
        name="collect",
    )
    keys, attn, passed, stats = call(
        forward_kernel,
        [place_info, bounds, begins, key_pos, *over_rows(own_keys), queries, grads],
        [SMEM] * 2 + [VMEM] * 8,
        [shape((LENGTH, 2 * HD), BF), shape((quarter, HD), F32), rows_one, shape((8, quarter), F32)],
        [pltpu.VMEM((quarter + ROWS, HD), F32)] + work_scratch(),
        flops=6 * 10**9,
        name="forward",
    )
    all_queries = over_rows(queries)
    (d_attn,) = call(
        attn_grad_kernel,
        [*to_heads([stats] * 4), attn, grads, *all_queries[1:]],
        [VMEM] * 6 + [pl.BlockSpec(memory_space=pl.ANY)] * 3,
        [rows_one],
        flops=10**9,
        name="attn_grad",
    )
    all_d_attn = over_rows(d_attn)
    (d_query,) = call(
        query_grad_kernel,
        [place_info, bounds, begins, key_pos, keys, queries, d_attn],
        [SMEM] * 2 + [VMEM] * 5,
        [rows_one],
        [pltpu.VMEM((quarter + ROWS, HD), F32)] + work_scratch(),
        flops=6 * 10**9,
        name="query_grad",
    )
    back_parts = call(
        key_grad_kernel,
        [place_info, bounds, starts, query_pos, own_keys, *all_queries, *all_d_attn, d_query, attn],
        [SMEM] * 2 + [VMEM] * 13,
        [four] * 4,
        [pltpu.VMEM((LENGTH, HD), BF), pltpu.VMEM((LENGTH, HD), BF), pltpu.VMEM((quarter + ROWS, 2 * HD), F32)]
        + work_scratch(),
        flops=7 * 10**9,
        name="key_grad",
    )
    incoming = output_gradient[0]
    *returning, mixed = call(
        input_grad_kernel,
        [place_info, dest, slot, *to_owners(back_parts), pre, dmixed, hist, incoming, w_in],
        [SMEM] * 3 + [VMEM] * 9,
        [block_shape] * 8 + [shape((ROWS, WIDTH), BF)],
        [
            pltpu.VMEM((ROWS, WIDTH), F32),
            pltpu.VMEM((ROWS, 3 * WIDTH), F32),
            pltpu.VMEM((ROWS, WIDTH), BF),
        ],
        flops=8 * ROWS * WIDTH * WIDTH,
        name="input_grad",
    )
    (layer_out,) = call(
        output_kernel,
        [mixed, hist, w_out],
        [VMEM] * 3,
        [shape((ROWS, WIDTH), BF)],
        flops=2 * ROWS * WIDTH * WIDTH,
        name="output",
    )
    came_back = [returning[0]] + [send(returning[k], back(tab_pairs(k))) for k in range(1, 8)]
    (table_grad,) = call(
        table_grad_kernel,
        [place_info, dest, row_ids.reshape(1, ROWS), *came_back],
        [SMEM, SMEM] + [VMEM] * 9,
        [shape((1, 1, tab_rows, WIDTH), BF)],
        [
            pltpu.VMEM((ROWS, WIDTH), BF),
            pltpu.VMEM((tiles, tile, WIDTH), BF),
            pltpu.SemaphoreType.DMA((tiles,)),
        ],
        flops=2 * ROWS * tab_rows * WIDTH,
        name="table_grad",
        out_specs=[pl.BlockSpec(memory_space=pltpu.HBM)],
    )
    return layer_out.reshape(1, ROWS, WIDTH), table_grad


def solution(mesh):
    fine = Mesh(mesh.devices.reshape(4, 4, 4, 2), AXES)
    ctx, tab = ("x", "z"), ("y", "c")
    in_specs = (
        P(ctx, tab, None, None),
        P(ctx, tab, None),
        P(ctx, None, None),
        P(ctx, None, None),
        P(tab, None),
        P(tab, None, None),
        P(),
        P(),
        P(tab, ctx, None),
    )
    out_specs = (P(tab, ctx, None), P(ctx, tab, None, None))
    return jax.shard_map(body, mesh=fine, in_specs=in_specs, out_specs=out_specs, check_vma=False)
```

```python
import functools

import jax
import jax.numpy as jnp
from jax import lax
from jax.experimental import pallas as pl
from jax.experimental.pallas import tpu as pltpu
from jax.sharding import Mesh, PartitionSpec as P

HEADS = 4
BROWS = 64
NBLK = 4
WIDTH = 512
HD = 128
ROWS = 256
CHUNK = 128
LENGTH = 4096
EPS = 1e-05
BF = jnp.bfloat16
F32 = jnp.float32
AXES = ("x", "z", "y", "c")
FAR = 1e9
KEY_TILE = 256
GROUP = 4
KEY_GROUP = 3
SINGLES = 8
ITEMS = 128
SCALE = HD ** (-0.5)


def device_id(x, z, y, c):
    return ((x * 4 + z) * 4 + y) * 2 + c


def all_coords():
    return [(x, z, y, c) for x in range(4) for z in range(4) for y in range(4) for c in range(2)]


def tab_pairs(step):
    out = []
    for x, z, y, c in all_coords():
        y2, c2 = divmod((y * 2 + c + step) % 8, 2)
        out.append((device_id(x, z, y, c), device_id(x, z, y2, c2)))
    return out


def moved(axis, step):
    out = []
    for x, z, y, c in all_coords():
        to = ((x + step) % 4, z) if axis == c else (x, (z + step) % 4)
        out.append((device_id(x, z, y, c), device_id(*to, y, c)))
    return out


def head_pairs(step):
    return moved(0, step)


def row_pairs(step):
    return moved(1, step)


def back(pairs):
    return [(b, a) for a, b in pairs]


def send(value, pairs):
    return lax.ppermute(value, AXES, pairs)


def dot(a, b):
    return jnp.dot(a, b, preferred_element_type=F32)


def dot_nt(a, b):
    return lax.dot_general(a, b, (((1,), (1,)), ((), ())), preferred_element_type=F32)


def silu(z):
    h = 0.5 * z
    return h + h * jnp.tanh(h)


def silu_slope(z):
    h = 0.5 * z
    t = jnp.tanh(h)
    return 0.5 * (1.0 + t) * (1.0 + h * (1.0 - t))


def row_statistics(x):
    mean = jnp.mean(x, axis=-1, keepdims=True)
    centred = x - mean
    inverse = lax.rsqrt(jnp.mean(centred * centred, axis=-1, keepdims=True) + EPS)
    return centred * inverse, inverse


def norm_backward(grad, hat, inverse):
    first = jnp.mean(grad, axis=-1, keepdims=True)
    second = jnp.mean(grad * hat, axis=-1, keepdims=True)
    return inverse * (grad - first - hat * second)


def column_of(row):
    return jnp.transpose(jnp.broadcast_to(row, (CHUNK, CHUNK)))


def ds(start, size):
    return pl.ds(pl.multiple_of(start, size), size)


VMEM = pl.BlockSpec(memory_space=pltpu.VMEM)
SMEM = pl.BlockSpec(memory_space=pltpu.SMEM)


def shape(dims, dtype):
    return jax.ShapeDtypeStruct(dims, dtype)


def call(kernel, ins, specs, outs, scratch=(), flops=0, name=None, out_specs=None, limit=40, placed=True):
    moved = sum(a.size * a.dtype.itemsize for a in ins)
    moved += sum(o.size * jnp.dtype(o.dtype).itemsize for o in outs)
    return pl.pallas_call(
        with_place(kernel) if placed else kernel,
        out_shape=outs,
        in_specs=specs,
        out_specs=out_specs or [VMEM] * len(outs),
        scratch_shapes=list(scratch),
        compiler_params=pltpu.CompilerParams(vmem_limit_bytes=limit * 1024 * 1024),
        cost_estimate=pl.CostEstimate(flops=flops, bytes_accessed=moved, transcendentals=0),
        name=name,
    )(*ins)


def with_place(kernel):
    def placed(*refs):
        kernel([lax.axis_index(a) for a in AXES], *refs)

    return placed


def lookup_kernel(meta, dest, ids_ref, table, *rest):
    outs, (buffer, total, column, arrived) = rest[:8], rest[8:]
    tile = buffer.shape[1]
    copies = [
        pltpu.make_async_copy(table.at[0, 0, pl.ds(n * tile, tile), :], buffer.at[n], arrived.at[n])
        for n in range(buffer.shape[0])
    ]
    for copy in copies:
        copy.start()
    for b in range(2):
        column[b * CHUNK : (b + 1) * CHUNK, :] = column_of(ids_ref[b : b + 1, :].astype(F32))
    lane = lax.broadcasted_iota(jnp.int32, (ROWS, CHUNK), 1).astype(F32)
    for n, copy in enumerate(copies):
        hits = [
            jnp.where(column[...] == lane + float(n * tile + m * CHUNK), 1.0, 0.0).astype(BF)
            for m in range(tile // CHUNK)
        ]
        copy.wait()
        part = dot(jnp.concatenate(hits, axis=1), buffer[n])
        if n == 0:
            total[...] = part
        else:
            total[...] += part
    own = meta[2] * 2 + meta[3]
    for k in range(8):
        outs[k][...] = jnp.zeros_like(outs[k])
        for p in range(NBLK):

            @pl.when(dest[p, own] == lax.rem(own + k, 8))
            def _():
                outs[k][...] = total[p * BROWS : (p + 1) * BROWS, :].astype(BF)


def prepare_kernel(meta, lengths, tile_mask, incoming, w_out, key_work, query_work, starts, begins, key_pos, query_pos, dmixed, turned, bounds):
    row, core = line(meta)[1], meta[3]
    ends, end = [], jnp.int32(0)
    for d in range(lengths.shape[0]):
        end = end + lengths[d]
        ends.append(end)
    for t in range(8):
        i = chunk_of(t, row, core)
        begin, stop = jnp.int32(0), jnp.int32(LENGTH)
        for end in ends:
            begin = jnp.where(i * CHUNK >= end, end, begin)
        for end in reversed(ends):
            stop = jnp.where(i * CHUNK + CHUNK - 1 < end, end, stop)
        bounds[t] = begin
        bounds[8 + t] = stop - 1

    def key_span(t):
        i = chunk_of(t, row, core)
        return bounds[t] // KEY_TILE, (i * CHUNK + CHUNK - 1) // KEY_TILE

    def query_span(t):
        i = chunk_of(t, row, core)
        return (i * CHUNK) // KEY_TILE, bounds[8 + t] // KEY_TILE

    list_work(key_work, key_span, core)
    list_work(query_work, query_span, core)
    turned[...] = jnp.transpose(tile_mask[...].astype(F32))
    on_keys, on_queries = [], []
    for t in range(8):
        i = chunk_of(t, row, core)
        position = lax.broadcasted_iota(jnp.int32, (CHUNK, CHUNK), 0) + i * CHUNK
        begin = jnp.zeros((CHUNK, CHUNK), jnp.int32)
        for end in ends:
            begin = jnp.where(position >= end, end, begin)
        begins[t * CHUNK : (t + 1) * CHUNK, :] = begin.astype(F32)
        for m in range(2):
            on_keys.append(tile_mask[pl.ds(2 * i + m, 1), :])
            on_queries.append(turned[pl.ds(2 * i + m, 1), :])
    on_keys = jnp.concatenate(on_keys, axis=0).astype(F32).astype(BF)
    on_queries = jnp.concatenate(on_queries, axis=0).astype(BF)
    for n in range(8):
        cols = slice(n * WIDTH, (n + 1) * WIDTH)
        spot = lax.broadcasted_iota(jnp.int32, (BROWS, WIDTH), 1) + n * WIDTH
        pick = jnp.where(
            lax.broadcasted_iota(jnp.int32, (BROWS, WIDTH), 0) == spot // BROWS, 1.0, 0.0
        ).astype(BF)
        spot = spot[0:16, :]
        place = spot.astype(F32)
        key_pos[:, cols] = jnp.where(dot(on_keys, pick) > 0.5, place, FAR)
        query_pos[:, cols] = jnp.where(dot(on_queries, pick) > 0.5, place, -1.0)
        spot = spot[0:8, :]
        begin = jnp.zeros((8, WIDTH), jnp.int32)
        for end in ends:
            begin = jnp.where(spot >= end, end, begin)
        starts[:, cols] = begin.astype(F32)
    dmixed[...] = dot_nt(incoming[...], w_out[...])


def project_kernel(meta, dest, slot, *rest):
    blocks, (w_ref, dmixed_ref), rest = rest[:8], rest[8:10], rest[10:]
    hist, pre = rest[:2]
    outs = rest[2:6]
    act, grads = rest[6:]
    own = meta[2] * 2 + meta[3]
    for k in range(8):
        source = lax.rem(own - k + 8, 8)
        for p in range(NBLK):

            @pl.when(dest[p, source] == own)
            def _():
                hist[ds(slot[p, source] * BROWS, BROWS), :] = blocks[k][...]

    hat, _ = row_statistics(hist[...].astype(F32))
    normed = hat.astype(BF)
    for n in range(4):
        cols = slice(n * WIDTH, (n + 1) * WIDTH)
        part = dot(normed, w_ref[:, cols])
        pre[:, cols] = part
        act[:, cols] = silu(part).astype(BF)
    grads[...] = (dmixed_ref[...] * act[:, 0:WIDTH].astype(F32)).astype(BF)
    for j in range(4):
        head = lax.rem(line(meta)[0] + j, 4) * HD
        outs[j][:, 0:HD] = act[:, ds(3 * WIDTH + head, HD)]
        outs[j][:, HD : 2 * HD] = act[:, ds(WIDTH + head, HD)]
        outs[j][:, 2 * HD : 3 * HD] = act[:, ds(2 * WIDTH + head, HD)]
        outs[j][:, 3 * HD : 4 * HD] = grads[:, ds(head, HD)]


def line(meta):
    first = meta[3] == 0
    return jnp.where(first, meta[0], meta[1]), jnp.where(first, meta[1], meta[0])


def chunk_of(t, row, core):
    spread = 4 * t + jnp.where(t < 4, row, 3 - row)
    solid = t + jnp.where(t < 4, 4 * row, 24 - 4 * row)
    return jnp.where(core == 0, spread, solid)


def pieces_of(meta):
    head = line(meta)[0]
    for j in range(4):
        source = lax.rem(head - j + 4, 4)
        yield j, 0, source
        yield j, CHUNK, 7 - source


def collect_kernel(meta, p0, p1, p2, p3, keys, queries, grads):
    pieces = (p0, p1, p2, p3)
    for j, low, t in pieces_of(meta):
        rows, part = ds(t * CHUNK, CHUNK), pieces[j]
        keys[rows, :] = part[low : low + CHUNK, 0 : 2 * HD]
        queries[rows, :] = part[low : low + CHUNK, 2 * HD : 3 * HD]
        grads[rows, :] = part[low : low + CHUNK, 3 * HD : 4 * HD]


def place_rows(meta, parts, out):
    row, core = line(meta)[1], meta[3]
    for k in range(4):
        other = lax.rem(row - k + 4, 4)
        for t in range(8):
            chunk = chunk_of(t, other, core)
            out[ds(chunk * CHUNK, CHUNK), :] = parts[k][t * CHUNK : (t + 1) * CHUNK, :]


def list_work(work, span, core):
    def put(unit):
        def one(n, count):
            work[count] = unit
            work[ITEMS + count] = n
            return count + 1

        return one

    def one_pair(p, count):
        low, high = span(2 * p)
        low_next, high_next = span(2 * p + 1)

        def together(count):
            count = lax.fori_loop(low, high + 1, put(p), count)
            return lax.fori_loop(jnp.maximum(low_next, high + 1), high_next + 1, put(p), count)

        def alone(count):
            count = lax.fori_loop(low, high + 1, put(2 * p), count)
            return lax.fori_loop(low_next, high_next + 1, put(2 * p + 1), count)

        return lax.cond(core == 0, alone, together, count)

    count = lax.fori_loop(0, 4, one_pair, jnp.int32(0))
    for u in range(SINGLES):
        work[count + u] = jnp.where(core == 0, 8, 4)
        work[ITEMS + count + u] = 0
    work[2 * ITEMS] = count


def run_items(work, core, item, size):
    def run(group_size, rows, last):
        def group(b, carry):
            done = []
            for u in range(group_size):
                slot, n = work[b * group_size + u], work[ITEMS + b * group_size + u]
                done.append((slot, item(jnp.minimum(slot, last), n, rows)))
            for slot, parts in done:
                for ref, cols, part in parts:
                    ref[ds(slot * rows, rows), cols] += part
            return carry

        lax.fori_loop(0, (work[2 * ITEMS] + group_size - 1) // group_size, group, 0)

    @pl.when(core == 0)
    def _():
        run(SINGLES, CHUNK, 7)

    @pl.when(core != 0)
    def _():
        run(size, ROWS, 3)


def unit_positions(meta, unit, rows, width):
    row, core = line(meta)[1], meta[3]
    local = lax.broadcasted_iota(jnp.int32, (CHUNK, width), 0).astype(F32)
    count = rows // CHUNK
    return jnp.concatenate(
        [local + (chunk_of(count * unit + m, row, core) * CHUNK).astype(F32) for m in range(count)], axis=0
    )


def spread_rows(table, unit, rows, cols):
    count = rows // BROWS
    return jnp.concatenate(
        [jnp.broadcast_to(table[pl.ds(count * unit + m, 1), cols], (BROWS, KEY_TILE)) for m in range(count)],
        axis=0,
    )


def allowed_keys(meta, begins, key_pos, unit, n, rows):
    repeat = KEY_TILE // CHUNK
    pos = jnp.concatenate([unit_positions(meta, unit, rows, CHUNK)] * repeat, axis=1)
    start = jnp.concatenate([begins[ds(unit * rows, rows), :]] * repeat, axis=1)
    key = spread_rows(key_pos, unit, rows, ds(n * KEY_TILE, KEY_TILE))
    return (key >= start) & (key <= pos)


def forward_kernel(
    meta, work, begins, key_pos, k0, k1, k2, k3, queries, grads, keys, attn, stats, total
):
    place_rows(meta, (k0, k1, k2, k3), keys)
    total[...] = jnp.zeros_like(total)

    def item(unit, n, rows):
        near = ds(n * KEY_TILE, KEY_TILE)
        h = dot_nt(queries[ds(unit * rows, rows), :], keys[near, 0:HD]) * (0.5 * SCALE)
        allowed = allowed_keys(meta, begins, key_pos, unit, n, rows)
        probs = jnp.where(allowed, h + h * jnp.tanh(h), 0.0).astype(BF)
        return [(total, slice(None), dot(probs, keys[near, HD : 2 * HD]))]

    run_items(work, meta[3], item, GROUP)
    lane = lax.broadcasted_iota(jnp.int32, (CHUNK, CHUNK), 1)
    for t in range(8):
        rows = slice(t * CHUNK, (t + 1) * CHUNK)
        x = total[rows, :]
        attn[rows, :] = x
        e = grads[rows, :].astype(F32)
        mean = jnp.mean(x, axis=1, keepdims=True)
        centred = x - mean
        packed = jnp.where(lane == 0, mean, 0.0)
        packed = jnp.where(lane == 1, jnp.sum(centred * centred, axis=1, keepdims=True), packed)
        packed = jnp.where(lane == 2, jnp.sum(e, axis=1, keepdims=True), packed)
        packed = jnp.where(lane == 3, jnp.sum(e * centred, axis=1, keepdims=True), packed)
        stats[:, rows] = jnp.transpose(packed)[0:8, :]


def attn_grad_kernel(s0, s1, s2, s3, attn, grads, q1, q2, q3, out):
    parts = [s[...] for s in (s0, s1, s2, s3)]
    means = [s[0:1, :] for s in parts]
    mean = (means[0] + means[1] + means[2] + means[3]) * 0.25
    spread = sum(s[1:2, :] + HD * (m - mean) * (m - mean) for s, m in zip(parts, means))
    inverse = lax.rsqrt(spread * (1.0 / WIDTH) + EPS)
    e_mean = sum(s[2:3, :] for s in parts) * (1.0 / WIDTH)
    e_on = sum(s[3:4, :] + (m - mean) * s[2:3, :] for s, m in zip(parts, means))
    e_on = e_on * inverse * (1.0 / WIDTH)
    for t in range(8):
        rows = slice(t * CHUNK, (t + 1) * CHUNK)
        cols = [column_of(v[:, rows]) for v in (mean, inverse, e_mean, e_on)]
        hat = (attn[rows, :] - cols[0]) * cols[1]
        out[rows, :] = (cols[1] * (grads[rows, :].astype(F32) - cols[2] - hat * cols[3])).astype(BF)


def query_grad_kernel(meta, work, begins, key_pos, keys, queries, d_attn, out, total):
    total[...] = jnp.zeros_like(total)

    def item(unit, n, rows):
        near = ds(n * KEY_TILE, KEY_TILE)
        own = ds(unit * rows, rows)
        k = keys[near, 0:HD]
        h = dot_nt(queries[own, :], k) * (0.5 * SCALE)
        dp = dot_nt(d_attn[own, :], keys[near, HD : 2 * HD])
        th = jnp.tanh(h)
        allowed = allowed_keys(meta, begins, key_pos, unit, n, rows)
        d_scores = jnp.where(allowed, dp * ((1.0 + th) * (1.0 + h - h * th)), 0.0)
        return [(total, slice(None), dot(d_scores.astype(BF), k))]

    run_items(work, meta[3], item, GROUP)
    out[...] = (total[0 : LENGTH // 4, :] * (0.5 * SCALE)).astype(BF)


def key_grad_kernel(
    meta, work, starts, query_pos, keys, q0, q1, q2, q3, g0, g1, g2, g3, d_query, attn,
    r0, r1, r2, r3, queries, grads, total,
):
    outs = (r0, r1, r2, r3)
    place_rows(meta, (q0, q1, q2, q3), queries)
    place_rows(meta, (g0, g1, g2, g3), grads)
    total[...] = jnp.zeros_like(total)

    def item(unit, n, rows):
        own = ds(unit * rows, rows)
        near = ds(n * KEY_TILE, KEY_TILE)
        q, g = queries[near, :], grads[near, :]
        pos = unit_positions(meta, unit, rows, KEY_TILE)
        begin = jnp.broadcast_to(starts[0:1, near], (rows, KEY_TILE))
        allowed = (pos <= spread_rows(query_pos, unit, rows, near)) & (pos >= begin)
        h = dot_nt(keys[own, 0:HD], q) * (0.5 * SCALE)
        dp = dot_nt(keys[own, HD : 2 * HD], g)
        th = jnp.tanh(h)
        up = 1.0 + th
        probs = jnp.where(allowed, h * up, 0.0).astype(BF)
        d_scores = jnp.where(allowed, dp * (up * (1.0 + h - h * th)), 0.0).astype(BF)
        return [
            (total, slice(0, HD), dot(d_scores, q)),
            (total, slice(HD, 2 * HD), dot(probs, g)),
        ]

    run_items(work, meta[3], item, KEY_GROUP)
    for j, low, t in pieces_of(meta):
        rows = ds(t * CHUNK, CHUNK)
        outs[j][low : low + CHUNK, 0:HD] = (total[rows, 0:HD] * (0.5 * SCALE)).astype(BF)
        outs[j][low : low + CHUNK, HD : 2 * HD] = total[rows, HD : 2 * HD].astype(BF)
        outs[j][low : low + CHUNK, 2 * HD : 3 * HD] = d_query[rows, :]
        outs[j][low : low + CHUNK, 3 * HD : 4 * HD] = attn[rows, :].astype(BF)


def input_grad_kernel(meta, dest, slot, p0, p1, p2, p3, pre, dmixed, hist, incoming, w_in, *rest):
    outs, (mixed, attn, d_act, result) = rest[:8], rest[8:]
    for j, part in enumerate((p0, p1, p2, p3)):
        head = lax.rem(line(meta)[0] + j, 4) * HD
        d_act[:, ds(2 * WIDTH + head, HD)] = part[:, 0:HD].astype(F32)
        d_act[:, ds(head, HD)] = part[:, HD : 2 * HD].astype(F32)
        d_act[:, ds(WIDTH + head, HD)] = part[:, 2 * HD : 3 * HD].astype(F32)
        attn[:, ds(head, HD)] = part[:, 3 * HD : 4 * HD].astype(F32)
    on, _ = row_statistics(attn[...])
    u_pre = pre[:, 0:WIDTH]
    mixed[...] = (on * silu(u_pre).astype(BF).astype(F32)).astype(BF)
    total = dot_nt((dmixed[...] * on * silu_slope(u_pre)).astype(BF), w_in[:, 0:WIDTH])
    for n in range(3):
        cols = slice((n + 1) * WIDTH, (n + 2) * WIDTH)
        d_pre = (d_act[:, n * WIDTH : (n + 1) * WIDTH] * silu_slope(pre[:, cols])).astype(BF)
        total = total + dot_nt(d_pre, w_in[:, cols])
    hat, inverse = row_statistics(hist[...].astype(F32))
    result[...] = (incoming[...].astype(F32) + norm_backward(total, hat, inverse)).astype(BF)
    own = meta[2] * 2 + meta[3]
    for k in range(8):
        outs[k][...] = jnp.zeros_like(outs[k])
        source = lax.rem(own - k + 8, 8)
        for p in range(NBLK):

            @pl.when(dest[p, source] == own)
            def _():
                outs[k][...] = result[ds(slot[p, source] * BROWS, BROWS), :]


def output_kernel(mixed, hist, w_out, out):
    out[...] = (hist[...].astype(F32) + dot(mixed[...], w_out[...])).astype(BF)


def table_grad_kernel(meta, dest, ids, *rest):
    blocks, out, rows, buffer, sent = rest[:8], rest[8], rest[9], rest[10], rest[11]
    tile = buffer.shape[1]
    own = meta[2] * 2 + meta[3]
    for k in range(8):
        for p in range(NBLK):

            @pl.when(dest[p, own] == lax.rem(own + k, 8))
            def _():
                rows[p * BROWS : (p + 1) * BROWS, :] = blocks[k][...]

    number = lax.broadcasted_iota(jnp.int32, (tile, ROWS), 0)
    copies = []
    for n in range(buffer.shape[0]):
        hits = jnp.where(number + n * tile == ids[...], 1.0, 0.0).astype(BF)
        buffer[n] = dot(hits, rows[...]).astype(BF)
        copy = pltpu.make_async_copy(buffer.at[n], out.at[0, 0, pl.ds(n * tile, tile), :], sent.at[n])
        copy.start()
        copies.append(copy)
    for copy in copies:
        copy.wait()


def body(table, row_ids, dests, slots, lengths, tile_mask, w_in, w_out, output_gradient):
    dest = dests[0].T
    slot = slots[0].T
    tab_rows = table.shape[2]

    key_work, query_work, starts, begins, key_pos, query_pos, dmixed = call(
        prepare_kernel,
        [lengths[0], tile_mask[0], output_gradient[0], w_out],
        [SMEM] + [VMEM] * 3,
        [
            shape((2 * ITEMS + 1,), jnp.int32),
            shape((2 * ITEMS + 1,), jnp.int32),
            shape((8, LENGTH), F32),
            shape((LENGTH // 4, CHUNK), F32),
            shape((16, LENGTH), F32),
            shape((16, LENGTH), F32),
            shape((ROWS, WIDTH), F32),
        ],
        [pltpu.VMEM((64, 64), F32), pltpu.SMEM((16,), jnp.int32)],
        flops=2 * ROWS * WIDTH * WIDTH,
        name="prepare",
        out_specs=[SMEM] * 2 + [VMEM] * 5,
    )

    tiles = 8
    tile = tab_rows // tiles
    block_shape = shape((BROWS, WIDTH), BF)
    outgoing = call(
        lookup_kernel,
        [dest, row_ids.reshape(2, CHUNK), table],
        [SMEM, VMEM, pl.BlockSpec(memory_space=pltpu.HBM)],
        [block_shape] * 8,
        [
            pltpu.VMEM((tiles, tile, WIDTH), BF),
            pltpu.VMEM((ROWS, WIDTH), F32),
            pltpu.VMEM((ROWS, CHUNK), F32),
            pltpu.SemaphoreType.DMA((tiles,)),
        ],
        flops=2 * ROWS * tab_rows * WIDTH,
        name="lookup",
        limit=60,
    )
    blocks = [outgoing[0]] + [send(outgoing[k], tab_pairs(k)) for k in range(1, 8)]

    four = shape((ROWS, 4 * HD), BF)
    two = shape((ROWS, 2 * HD), BF)
    one = shape((ROWS, HD), BF)
    quarter = LENGTH // 4
    rows_two = shape((quarter, 2 * HD), BF)
    rows_one = shape((quarter, HD), BF)

    def to_heads(values):
        return [values[0]] + [send(values[j], head_pairs(j)) for j in range(1, 4)]

    def to_owners(values):
        return [values[0]] + [send(values[j], back(head_pairs(j))) for j in range(1, 4)]

    def over_rows(value):
        return [value] + [send(value, row_pairs(k)) for k in range(1, 4)]

    hist, pre, *pieces = call(
        project_kernel,
        [dest, slot, *blocks, w_in, dmixed],
        [SMEM] * 2 + [VMEM] * 10,
        [shape((ROWS, WIDTH), BF), shape((ROWS, 4 * WIDTH), F32)] + [four] * 4,
        [pltpu.VMEM((ROWS, 4 * WIDTH), BF), pltpu.VMEM((ROWS, WIDTH), BF)],
        flops=2 * ROWS * WIDTH * 4 * WIDTH,
        name="project",
    )
    own_keys, queries, grads = call(
        collect_kernel,
        [*to_heads(pieces)],
        [VMEM] * 4,
        [rows_two, rows_one, rows_one],
        name="collect",
    )
    keys, attn, stats = call(
        forward_kernel,
        [key_work, begins, key_pos, *over_rows(own_keys), queries, grads],
        [SMEM] + [VMEM] * 8,
        [shape((LENGTH, 2 * HD), BF), shape((quarter, HD), F32), shape((8, quarter), F32)],
        [pltpu.VMEM((quarter + ROWS, HD), F32)],
        flops=6 * 10**9,
        name="forward",
    )
    all_queries = over_rows(queries)
    (d_attn,) = call(
        attn_grad_kernel,
        [*to_heads([stats] * 4), attn, grads, *all_queries[1:]],
        [VMEM] * 6 + [pl.BlockSpec(memory_space=pl.ANY)] * 3,
        [rows_one],
        flops=10**9,
        name="attn_grad",
        placed=False,
    )
    all_d_attn = over_rows(d_attn)
    (d_query,) = call(
        query_grad_kernel,
        [key_work, begins, key_pos, keys, queries, d_attn],
        [SMEM] + [VMEM] * 5,
        [rows_one],
        [pltpu.VMEM((quarter + ROWS, HD), F32)],
        flops=6 * 10**9,
        name="query_grad",
    )
    back_parts = call(
        key_grad_kernel,
        [query_work, starts, query_pos, own_keys, *all_queries, *all_d_attn, d_query, attn],
        [SMEM] + [VMEM] * 13,
        [four] * 4,
        [pltpu.VMEM((LENGTH, HD), BF), pltpu.VMEM((LENGTH, HD), BF), pltpu.VMEM((quarter + ROWS, 2 * HD), F32)]
       ,
        flops=7 * 10**9,
        name="key_grad",
    )
    incoming = output_gradient[0]
    *returning, mixed = call(
        input_grad_kernel,
        [dest, slot, *to_owners(back_parts), pre, dmixed, hist, incoming, w_in],
        [SMEM] * 2 + [VMEM] * 9,
        [block_shape] * 8 + [shape((ROWS, WIDTH), BF)],
        [
            pltpu.VMEM((ROWS, WIDTH), F32),
            pltpu.VMEM((ROWS, 3 * WIDTH), F32),
            pltpu.VMEM((ROWS, WIDTH), BF),
        ],
        flops=8 * ROWS * WIDTH * WIDTH,
        name="input_grad",
    )
    (layer_out,) = call(
        output_kernel,
        [mixed, hist, w_out],
        [VMEM] * 3,
        [shape((ROWS, WIDTH), BF)],
        flops=2 * ROWS * WIDTH * WIDTH,
        name="output",
        placed=False,
    )
    came_back = [returning[0]] + [send(returning[k], back(tab_pairs(k))) for k in range(1, 8)]
    (table_grad,) = call(
        table_grad_kernel,
        [dest, row_ids.reshape(1, ROWS), *came_back],
        [SMEM] + [VMEM] * 9,
        [shape((1, 1, tab_rows, WIDTH), BF)],
        [
            pltpu.VMEM((ROWS, WIDTH), BF),
            pltpu.VMEM((tiles, tile, WIDTH), BF),
            pltpu.SemaphoreType.DMA((tiles,)),
        ],
        flops=2 * ROWS * tab_rows * WIDTH,
        name="table_grad",
        out_specs=[pl.BlockSpec(memory_space=pltpu.HBM)],
    )
    return layer_out.reshape(1, ROWS, WIDTH), table_grad


def solution(mesh):
    fine = Mesh(mesh.devices.reshape(4, 4, 4, 2), AXES)
    ctx, tab = ("x", "z"), ("y", "c")
    in_specs = (
        P(ctx, tab, None, None),
        P(ctx, tab, None),
        P(ctx, None, None),
        P(ctx, None, None),
        P(tab, None),
        P(tab, None, None),
        P(),
        P(),
        P(tab, ctx, None),
    )
    out_specs = (P(tab, ctx, None), P(ctx, tab, None, None))
    return jax.shard_map(body, mesh=fine, in_specs=in_specs, out_specs=out_specs, check_vma=False)
```

```python
import functools

import jax
import jax.numpy as jnp
from jax import lax
from jax.experimental import pallas as pl
from jax.experimental.pallas import tpu as pltpu
from jax.sharding import Mesh, PartitionSpec as P

HEADS = 4
BROWS = 64
NBLK = 4
WIDTH = 512
HD = 128
ROWS = 256
CHUNK = 128
LENGTH = 4096
EPS = 1e-05
BF = jnp.bfloat16
F32 = jnp.float32
AXES = ("x", "z", "y", "c")
FAR = 1e9
KEY_TILE = 256
GROUP = 4
KEY_GROUP = 3
SINGLES = 8
ITEMS = 128
SCALE = HD ** (-0.5)


def device_id(x, z, y, c):
    return ((x * 4 + z) * 4 + y) * 2 + c


def all_coords():
    return [(x, z, y, c) for x in range(4) for z in range(4) for y in range(4) for c in range(2)]


def tab_pairs(step):
    out = []
    for x, z, y, c in all_coords():
        y2, c2 = divmod((y * 2 + c + step) % 8, 2)
        out.append((device_id(x, z, y, c), device_id(x, z, y2, c2)))
    return out


def chip_pairs(step):
    return [(device_id(x, z, y, c), device_id(x, z, (y + step) % 4, c)) for x, z, y, c in all_coords()]


def core_pairs():
    return [(device_id(x, z, y, c), device_id(x, z, y, 1 - c)) for x, z, y, c in all_coords()]


def moved(axis, step):
    out = []
    for x, z, y, c in all_coords():
        to = ((x + step) % 4, z) if axis == c else (x, (z + step) % 4)
        out.append((device_id(x, z, y, c), device_id(*to, y, c)))
    return out


def head_pairs(step):
    return moved(0, step)


def row_pairs(step):
    return moved(1, step)


def back(pairs):
    return [(b, a) for a, b in pairs]


def send(value, pairs):
    return lax.ppermute(value, AXES, pairs)


def dot(a, b):
    return jnp.dot(a, b, preferred_element_type=F32)


def dot_nt(a, b):
    return lax.dot_general(a, b, (((1,), (1,)), ((), ())), preferred_element_type=F32)


def silu(z):
    h = 0.5 * z
    return h + h * jnp.tanh(h)


def silu_slope(z):
    h = 0.5 * z
    t = jnp.tanh(h)
    return 0.5 * (1.0 + t) * (1.0 + h * (1.0 - t))


def row_statistics(x):
    mean = jnp.mean(x, axis=-1, keepdims=True)
    centred = x - mean
    inverse = lax.rsqrt(jnp.mean(centred * centred, axis=-1, keepdims=True) + EPS)
    return centred * inverse, inverse


def norm_backward(grad, hat, inverse):
    first = jnp.mean(grad, axis=-1, keepdims=True)
    second = jnp.mean(grad * hat, axis=-1, keepdims=True)
    return inverse * (grad - first - hat * second)


def column_of(row):
    return jnp.transpose(jnp.broadcast_to(row, (CHUNK, CHUNK)))


def ds(start, size):
    return pl.ds(pl.multiple_of(start, size), size)


VMEM = pl.BlockSpec(memory_space=pltpu.VMEM)
SMEM = pl.BlockSpec(memory_space=pltpu.SMEM)


def shape(dims, dtype):
    return jax.ShapeDtypeStruct(dims, dtype)


def call(kernel, ins, specs, outs, scratch=(), flops=0, name=None, out_specs=None, limit=40, placed=True):
    moved = sum(a.size * a.dtype.itemsize for a in ins)
    moved += sum(o.size * jnp.dtype(o.dtype).itemsize for o in outs)
    return pl.pallas_call(
        with_place(kernel) if placed else kernel,
        out_shape=outs,
        in_specs=specs,
        out_specs=out_specs or [VMEM] * len(outs),
        scratch_shapes=list(scratch),
        compiler_params=pltpu.CompilerParams(vmem_limit_bytes=limit * 1024 * 1024),
        cost_estimate=pl.CostEstimate(flops=flops, bytes_accessed=moved, transcendentals=0),
        name=name,
    )(*ins)


def with_place(kernel):
    def placed(*refs):
        kernel([lax.axis_index(a) for a in AXES], *refs)

    return placed


def lookup_kernel(meta, dest, ids_ref, table, *rest):
    outs, (buffer, total, column, arrived) = rest[:4], rest[4:]
    tile = buffer.shape[1]
    copies = [
        pltpu.make_async_copy(table.at[0, 0, pl.ds(n * tile, tile), :], buffer.at[n], arrived.at[n])
        for n in range(buffer.shape[0])
    ]
    for copy in copies:
        copy.start()
    for b in range(2):
        column[b * CHUNK : (b + 1) * CHUNK, :] = column_of(ids_ref[b : b + 1, :].astype(F32))
    lane = lax.broadcasted_iota(jnp.int32, (ROWS, CHUNK), 1).astype(F32)
    for n, copy in enumerate(copies):
        hits = [
            jnp.where(column[...] == lane + float(n * tile + m * CHUNK), 1.0, 0.0).astype(BF)
            for m in range(tile // CHUNK)
        ]
        copy.wait()
        part = dot(jnp.concatenate(hits, axis=1), buffer[n])
        if n == 0:
            total[...] = part
        else:
            total[...] += part
    own = meta[2] * 2 + meta[3]
    for k in range(4):
        for core in range(2):
            place = slice(core * BROWS, (core + 1) * BROWS)
            outs[k][place, :] = jnp.zeros((BROWS, WIDTH), BF)
            for p in range(NBLK):

                @pl.when(dest[p, own] == lax.rem(meta[2] + k, 4) * 2 + core)
                def _():
                    outs[k][place, :] = total[p * BROWS : (p + 1) * BROWS, :].astype(BF)


def prepare_kernel(
    meta, lengths, tile_mask, piece, key_work, query_work, starts, begins, key_pos, query_pos, passed, turned, bounds
):
    passed[...] = piece[...]
    row, core = line(meta)[1], meta[3]
    ends, end = [], jnp.int32(0)
    for d in range(lengths.shape[0]):
        end = end + lengths[d]
        ends.append(end)
    for t in range(8):
        i = chunk_of(t, row, core)
        begin, stop = jnp.int32(0), jnp.int32(LENGTH)
        for end in ends:
            begin = jnp.where(i * CHUNK >= end, end, begin)
        for end in reversed(ends):
            stop = jnp.where(i * CHUNK + CHUNK - 1 < end, end, stop)
        bounds[t] = begin
        bounds[8 + t] = stop - 1

    def key_span(t):
        i = chunk_of(t, row, core)
        return bounds[t] // KEY_TILE, (i * CHUNK + CHUNK - 1) // KEY_TILE

    def query_span(t):
        i = chunk_of(t, row, core)
        return (i * CHUNK) // KEY_TILE, bounds[8 + t] // KEY_TILE

    list_work(key_work, key_span, core)
    list_work(query_work, query_span, core)
    turned[...] = jnp.transpose(tile_mask[...].astype(F32))
    on_keys, on_queries = [], []
    for t in range(8):
        i = chunk_of(t, row, core)
        position = lax.broadcasted_iota(jnp.int32, (CHUNK, CHUNK), 0) + i * CHUNK
        begin = jnp.zeros((CHUNK, CHUNK), jnp.int32)
        for end in ends:
            begin = jnp.where(position >= end, end, begin)
        begins[t * CHUNK : (t + 1) * CHUNK, :] = begin.astype(F32)
        for m in range(2):
            on_keys.append(tile_mask[pl.ds(2 * i + m, 1), :])
            on_queries.append(turned[pl.ds(2 * i + m, 1), :])
    on_keys = jnp.concatenate(on_keys, axis=0).astype(F32).astype(BF)
    on_queries = jnp.concatenate(on_queries, axis=0).astype(BF)
    for n in range(8):
        cols = slice(n * WIDTH, (n + 1) * WIDTH)
        spot = lax.broadcasted_iota(jnp.int32, (BROWS, WIDTH), 1) + n * WIDTH
        pick = jnp.where(
            lax.broadcasted_iota(jnp.int32, (BROWS, WIDTH), 0) == spot // BROWS, 1.0, 0.0
        ).astype(BF)
        spot = spot[0:16, :]
        place = spot.astype(F32)
        key_pos[:, cols] = jnp.where(dot(on_keys, pick) > 0.5, place, FAR)
        query_pos[:, cols] = jnp.where(dot(on_queries, pick) > 0.5, place, -1.0)
        spot = spot[0:8, :]
        begin = jnp.zeros((8, WIDTH), jnp.int32)
        for end in ends:
            begin = jnp.where(spot >= end, end, begin)
        starts[:, cols] = begin.astype(F32)


def mix_kernel(incoming, w_out, dmixed):
    dmixed[...] = dot_nt(incoming[...], w_out[...])


def project_kernel(meta, dest, slot, *rest):
    blocks, (w_ref, dmixed_ref), rest = rest[:8], rest[8:10], rest[10:]
    hist, pre = rest[:2]
    outs = rest[2:6]
    act, grads = rest[6:]
    core = meta[3]
    own = meta[2] * 2 + core
    for k in range(8):
        source = lax.rem(meta[2] - k % 4 + 4, 4) * 2 + (core if k < 4 else 1 - core)
        for p in range(NBLK):

            @pl.when(dest[p, source] == own)
            def _():
                hist[ds(slot[p, source] * BROWS, BROWS), :] = blocks[k][ds(core * BROWS, BROWS), :]

    hat, _ = row_statistics(hist[...].astype(F32))
    normed = hat.astype(BF)
    for n in range(4):
        cols = slice(n * WIDTH, (n + 1) * WIDTH)
        part = dot(normed, w_ref[:, cols])
        pre[:, cols] = part
        act[:, cols] = silu(part).astype(BF)
    grads[...] = (dmixed_ref[...] * act[:, 0:WIDTH].astype(F32)).astype(BF)
    for j in range(4):
        head = lax.rem(line(meta)[0] + j, 4) * HD
        outs[j][:, 0:HD] = act[:, ds(3 * WIDTH + head, HD)]
        outs[j][:, HD : 2 * HD] = act[:, ds(WIDTH + head, HD)]
        outs[j][:, 2 * HD : 3 * HD] = act[:, ds(2 * WIDTH + head, HD)]
        outs[j][:, 3 * HD : 4 * HD] = grads[:, ds(head, HD)]


def line(meta):
    first = meta[3] == 0
    return jnp.where(first, meta[0], meta[1]), jnp.where(first, meta[1], meta[0])


def chunk_of(t, row, core):
    spread = 4 * t + jnp.where(t < 4, row, 3 - row)
    solid = t + jnp.where(t < 4, 4 * row, 24 - 4 * row)
    return jnp.where(core == 0, spread, solid)


def pieces_of(meta):
    head = line(meta)[0]
    for j in range(4):
        source = lax.rem(head - j + 4, 4)
        yield j, 0, source
        yield j, CHUNK, 7 - source


def collect_kernel(meta, p0, p1, p2, p3, keys, queries, grads):
    pieces = (p0, p1, p2, p3)
    for j, low, t in pieces_of(meta):
        rows, part = ds(t * CHUNK, CHUNK), pieces[j]
        keys[rows, :] = part[low : low + CHUNK, 0 : 2 * HD]
        queries[rows, :] = part[low : low + CHUNK, 2 * HD : 3 * HD]
        grads[rows, :] = part[low : low + CHUNK, 3 * HD : 4 * HD]


def place_rows(meta, parts, out):
    row, core = line(meta)[1], meta[3]
    for k in range(4):
        other = lax.rem(row - k + 4, 4)
        for t in range(8):
            chunk = chunk_of(t, other, core)
            out[ds(chunk * CHUNK, CHUNK), :] = parts[k][t * CHUNK : (t + 1) * CHUNK, :]


def list_work(work, span, core):
    def put(unit):
        def one(n, count):
            work[count] = unit
            work[ITEMS + count] = n
            return count + 1

        return one

    def one_pair(p, count):
        low, high = span(2 * p)
        low_next, high_next = span(2 * p + 1)

        def together(count):
            count = lax.fori_loop(low, high + 1, put(p), count)
            return lax.fori_loop(jnp.maximum(low_next, high + 1), high_next + 1, put(p), count)

        def alone(count):
            count = lax.fori_loop(low, high + 1, put(2 * p), count)
            return lax.fori_loop(low_next, high_next + 1, put(2 * p + 1), count)

        return lax.cond(core == 0, alone, together, count)

    count = lax.fori_loop(0, 4, one_pair, jnp.int32(0))
    for u in range(SINGLES):
        work[count + u] = jnp.where(core == 0, 8, 4)
        work[ITEMS + count + u] = 0
    work[2 * ITEMS] = count


def run_items(work, core, item, size):
    def run(group_size, rows, last):
        def group(b, carry):
            done = []
            for u in range(group_size):
                slot, n = work[b * group_size + u], work[ITEMS + b * group_size + u]
                done.append((slot, item(jnp.minimum(slot, last), n, rows)))
            for slot, parts in done:
                for ref, cols, part in parts:
                    ref[ds(slot * rows, rows), cols] += part
            return carry

        lax.fori_loop(0, (work[2 * ITEMS] + group_size - 1) // group_size, group, 0)

    @pl.when(core == 0)
    def _():
        run(SINGLES, CHUNK, 7)

    @pl.when(core != 0)
    def _():
        run(size, ROWS, 3)


def unit_positions(meta, unit, rows, width):
    row, core = line(meta)[1], meta[3]
    local = lax.broadcasted_iota(jnp.int32, (CHUNK, width), 0).astype(F32)
    count = rows // CHUNK
    return jnp.concatenate(
        [local + (chunk_of(count * unit + m, row, core) * CHUNK).astype(F32) for m in range(count)], axis=0
    )


def spread_rows(table, unit, rows, cols):
    count = rows // BROWS
    return jnp.concatenate(
        [jnp.broadcast_to(table[pl.ds(count * unit + m, 1), cols], (BROWS, KEY_TILE)) for m in range(count)],
        axis=0,
    )


def allowed_keys(meta, begins, key_pos, unit, n, rows):
    repeat = KEY_TILE // CHUNK
    pos = jnp.concatenate([unit_positions(meta, unit, rows, CHUNK)] * repeat, axis=1)
    start = jnp.concatenate([begins[ds(unit * rows, rows), :]] * repeat, axis=1)
    key = spread_rows(key_pos, unit, rows, ds(n * KEY_TILE, KEY_TILE))
    return (key >= start) & (key <= pos)


def forward_kernel(
    meta, work, begins, key_pos, k0, k1, k2, k3, queries, grads, keys, attn, stats, total
):
    place_rows(meta, (k0, k1, k2, k3), keys)
    total[...] = jnp.zeros_like(total)

    def item(unit, n, rows):
        near = ds(n * KEY_TILE, KEY_TILE)
        h = dot_nt(queries[ds(unit * rows, rows), :], keys[near, 0:HD]) * (0.5 * SCALE)
        allowed = allowed_keys(meta, begins, key_pos, unit, n, rows)
        probs = jnp.where(allowed, h + h * jnp.tanh(h), 0.0).astype(BF)
        return [(total, slice(None), dot(probs, keys[near, HD : 2 * HD]))]

    run_items(work, meta[3], item, GROUP)
    lane = lax.broadcasted_iota(jnp.int32, (CHUNK, CHUNK), 1)
    for t in range(8):
        rows = slice(t * CHUNK, (t + 1) * CHUNK)
        x = total[rows, :]
        attn[rows, :] = x
        e = grads[rows, :].astype(F32)
        mean = jnp.mean(x, axis=1, keepdims=True)
        centred = x - mean
        packed = jnp.where(lane == 0, mean, 0.0)
        packed = jnp.where(lane == 1, jnp.sum(centred * centred, axis=1, keepdims=True), packed)
        packed = jnp.where(lane == 2, jnp.sum(e, axis=1, keepdims=True), packed)
        packed = jnp.where(lane == 3, jnp.sum(e * centred, axis=1, keepdims=True), packed)
        stats[:, rows] = jnp.transpose(packed)[0:8, :]


def attn_grad_kernel(s0, s1, s2, s3, attn, grads, q1, q2, q3, out):
    parts = [s[...] for s in (s0, s1, s2, s3)]
    means = [s[0:1, :] for s in parts]
    mean = (means[0] + means[1] + means[2] + means[3]) * 0.25
    spread = sum(s[1:2, :] + HD * (m - mean) * (m - mean) for s, m in zip(parts, means))
    inverse = lax.rsqrt(spread * (1.0 / WIDTH) + EPS)
    e_mean = sum(s[2:3, :] for s in parts) * (1.0 / WIDTH)
    e_on = sum(s[3:4, :] + (m - mean) * s[2:3, :] for s, m in zip(parts, means))
    e_on = e_on * inverse * (1.0 / WIDTH)
    for t in range(8):
        rows = slice(t * CHUNK, (t + 1) * CHUNK)
        cols = [column_of(v[:, rows]) for v in (mean, inverse, e_mean, e_on)]
        hat = (attn[rows, :] - cols[0]) * cols[1]
        out[rows, :] = (cols[1] * (grads[rows, :].astype(F32) - cols[2] - hat * cols[3])).astype(BF)


def query_grad_kernel(meta, work, begins, key_pos, keys, queries, d_attn, out, total):
    total[...] = jnp.zeros_like(total)

    def item(unit, n, rows):
        near = ds(n * KEY_TILE, KEY_TILE)
        own = ds(unit * rows, rows)
        k = keys[near, 0:HD]
        h = dot_nt(queries[own, :], k) * (0.5 * SCALE)
        dp = dot_nt(d_attn[own, :], keys[near, HD : 2 * HD])
        th = jnp.tanh(h)
        allowed = allowed_keys(meta, begins, key_pos, unit, n, rows)
        d_scores = jnp.where(allowed, dp * ((1.0 + th) * (1.0 + h - h * th)), 0.0)
        return [(total, slice(None), dot(d_scores.astype(BF), k))]

    run_items(work, meta[3], item, GROUP)
    out[...] = (total[0 : LENGTH // 4, :] * (0.5 * SCALE)).astype(BF)


def key_grad_kernel(
    meta, work, starts, query_pos, keys, q0, q1, q2, q3, g0, g1, g2, g3, d_query, attn,
    r0, r1, r2, r3, queries, grads, total,
):
    outs = (r0, r1, r2, r3)
    place_rows(meta, (q0, q1, q2, q3), queries)
    place_rows(meta, (g0, g1, g2, g3), grads)
    total[...] = jnp.zeros_like(total)

    def item(unit, n, rows):
        own = ds(unit * rows, rows)
        near = ds(n * KEY_TILE, KEY_TILE)
        q, g = queries[near, :], grads[near, :]
        pos = unit_positions(meta, unit, rows, KEY_TILE)
        begin = jnp.broadcast_to(starts[0:1, near], (rows, KEY_TILE))
        allowed = (pos <= spread_rows(query_pos, unit, rows, near)) & (pos >= begin)
        h = dot_nt(keys[own, 0:HD], q) * (0.5 * SCALE)
        dp = dot_nt(keys[own, HD : 2 * HD], g)
        th = jnp.tanh(h)
        up = 1.0 + th
        probs = jnp.where(allowed, h * up, 0.0).astype(BF)
        d_scores = jnp.where(allowed, dp * (up * (1.0 + h - h * th)), 0.0).astype(BF)
        return [
            (total, slice(0, HD), dot(d_scores, q)),
            (total, slice(HD, 2 * HD), dot(probs, g)),
        ]

    run_items(work, meta[3], item, KEY_GROUP)
    for j, low, t in pieces_of(meta):
        rows = ds(t * CHUNK, CHUNK)
        outs[j][low : low + CHUNK, 0:HD] = (total[rows, 0:HD] * (0.5 * SCALE)).astype(BF)
        outs[j][low : low + CHUNK, HD : 2 * HD] = total[rows, HD : 2 * HD].astype(BF)
        outs[j][low : low + CHUNK, 2 * HD : 3 * HD] = d_query[rows, :]
        outs[j][low : low + CHUNK, 3 * HD : 4 * HD] = attn[rows, :].astype(BF)


def input_grad_kernel(meta, dest, slot, p0, p1, p2, p3, pre, dmixed, hist, incoming, w_in, *rest):
    outs, (mixed, attn, d_act, result) = rest[:4], rest[4:]
    for j, part in enumerate((p0, p1, p2, p3)):
        head = lax.rem(line(meta)[0] + j, 4) * HD
        d_act[:, ds(2 * WIDTH + head, HD)] = part[:, 0:HD].astype(F32)
        d_act[:, ds(head, HD)] = part[:, HD : 2 * HD].astype(F32)
        d_act[:, ds(WIDTH + head, HD)] = part[:, 2 * HD : 3 * HD].astype(F32)
        attn[:, ds(head, HD)] = part[:, 3 * HD : 4 * HD].astype(F32)
    on, _ = row_statistics(attn[...])
    u_pre = pre[:, 0:WIDTH]
    mixed[...] = (on * silu(u_pre).astype(BF).astype(F32)).astype(BF)
    total = dot_nt((dmixed[...] * on * silu_slope(u_pre)).astype(BF), w_in[:, 0:WIDTH])
    for n in range(3):
        cols = slice((n + 1) * WIDTH, (n + 2) * WIDTH)
        d_pre = (d_act[:, n * WIDTH : (n + 1) * WIDTH] * silu_slope(pre[:, cols])).astype(BF)
        total = total + dot_nt(d_pre, w_in[:, cols])
    hat, inverse = row_statistics(hist[...].astype(F32))
    result[...] = (incoming[...].astype(F32) + norm_backward(total, hat, inverse)).astype(BF)
    own = meta[2] * 2 + meta[3]
    for k in range(4):
        for core in range(2):
            place = slice(core * BROWS, (core + 1) * BROWS)
            outs[k][place, :] = jnp.zeros((BROWS, WIDTH), BF)
            source = lax.rem(meta[2] - k + 4, 4) * 2 + core
            for p in range(NBLK):

                @pl.when(dest[p, source] == own)
                def _():
                    outs[k][place, :] = result[ds(slot[p, source] * BROWS, BROWS), :]


def output_kernel(mixed, hist, w_out, block, out, passed):
    passed[...] = block[...]
    out[...] = (hist[...].astype(F32) + dot(mixed[...], w_out[...])).astype(BF)


def table_grad_kernel(meta, dest, ids, *rest):
    blocks, out, rows, buffer, sent = rest[:8], rest[8], rest[9], rest[10], rest[11]
    tile = buffer.shape[1]
    core = meta[3]
    own = meta[2] * 2 + core
    for k in range(8):
        owner = lax.rem(meta[2] + k % 4, 4) * 2 + (core if k < 4 else 1 - core)
        for p in range(NBLK):

            @pl.when(dest[p, own] == owner)
            def _():
                rows[p * BROWS : (p + 1) * BROWS, :] = blocks[k][ds(core * BROWS, BROWS), :]

    number = lax.broadcasted_iota(jnp.int32, (tile, ROWS), 0)
    copies = []
    for n in range(buffer.shape[0]):
        hits = jnp.where(number + n * tile == ids[...], 1.0, 0.0).astype(BF)
        buffer[n] = dot(hits, rows[...]).astype(BF)
        copy = pltpu.make_async_copy(buffer.at[n], out.at[0, 0, pl.ds(n * tile, tile), :], sent.at[n])
        copy.start()
        copies.append(copy)
    for copy in copies:
        copy.wait()


def body(table, row_ids, dests, slots, lengths, tile_mask, w_in, w_out, output_gradient):
    dest = dests[0].T
    slot = slots[0].T
    tab_rows = table.shape[2]

    tiles = 8
    tile = tab_rows // tiles
    block_shape = shape((BROWS, WIDTH), BF)
    outgoing = call(
        lookup_kernel,
        [dest, row_ids.reshape(2, CHUNK), table],
        [SMEM, VMEM, pl.BlockSpec(memory_space=pltpu.HBM)],
        [shape((2 * BROWS, WIDTH), BF)] * 4,
        [
            pltpu.VMEM((tiles, tile, WIDTH), BF),
            pltpu.VMEM((ROWS, WIDTH), F32),
            pltpu.VMEM((ROWS, CHUNK), F32),
            pltpu.SemaphoreType.DMA((tiles,)),
        ],
        flops=2 * ROWS * tab_rows * WIDTH,
        name="lookup",
        limit=60,
    )
    near = [outgoing[0]] + [send(outgoing[k], chip_pairs(k)) for k in range(1, 4)]
    blocks = near + [send(v, core_pairs()) for v in near]

    (dmixed,) = call(
        mix_kernel,
        [output_gradient[0], w_out],
        [VMEM] * 2,
        [shape((ROWS, WIDTH), F32)],
        flops=10**9,
        name="mix",
        placed=False,
    )

    four = shape((ROWS, 4 * HD), BF)
    two = shape((ROWS, 2 * HD), BF)
    one = shape((ROWS, HD), BF)
    quarter = LENGTH // 4
    rows_two = shape((quarter, 2 * HD), BF)
    rows_one = shape((quarter, HD), BF)

    def to_heads(values):
        return [values[0]] + [send(values[j], head_pairs(j)) for j in range(1, 4)]

    def to_owners(values):
        return [values[0]] + [send(values[j], back(head_pairs(j))) for j in range(1, 4)]

    def over_rows(value):
        return [value] + [send(value, row_pairs(k)) for k in range(1, 4)]

    hist, pre, *pieces = call(
        project_kernel,
        [dest, slot, *blocks, w_in, dmixed],
        [SMEM] * 2 + [VMEM] * 10,
        [shape((ROWS, WIDTH), BF), shape((ROWS, 4 * WIDTH), F32)] + [four] * 4,
        [pltpu.VMEM((ROWS, 4 * WIDTH), BF), pltpu.VMEM((ROWS, WIDTH), BF)],
        flops=2 * ROWS * WIDTH * 4 * WIDTH,
        name="project",
    )
    key_work, query_work, starts, begins, key_pos, query_pos, passed = call(
        prepare_kernel,
        [lengths[0], tile_mask[0], pieces[0]],
        [SMEM] + [VMEM] * 2,
        [
            shape((2 * ITEMS + 1,), jnp.int32),
            shape((2 * ITEMS + 1,), jnp.int32),
            shape((8, LENGTH), F32),
            shape((LENGTH // 4, CHUNK), F32),
            shape((16, LENGTH), F32),
            shape((16, LENGTH), F32),
            four,
        ],
        [pltpu.VMEM((64, 64), F32), pltpu.SMEM((16,), jnp.int32)],
        flops=3 * 10**9,
        name="prepare",
        out_specs=[SMEM] * 2 + [VMEM] * 5,
    )

    own_keys, queries, grads = call(
        collect_kernel,
        [passed, *to_heads(pieces)[1:]],
        [VMEM] * 4,
        [rows_two, rows_one, rows_one],
        name="collect",
    )
    keys, attn, stats = call(
        forward_kernel,
        [key_work, begins, key_pos, *over_rows(own_keys), queries, grads],
        [SMEM] + [VMEM] * 8,
        [shape((LENGTH, 2 * HD), BF), shape((quarter, HD), F32), shape((8, quarter), F32)],
        [pltpu.VMEM((quarter + ROWS, HD), F32)],
        flops=6 * 10**9,
        name="forward",
    )
    all_queries = over_rows(queries)
    (d_attn,) = call(
        attn_grad_kernel,
        [*to_heads([stats] * 4), attn, grads, *all_queries[1:]],
        [VMEM] * 6 + [pl.BlockSpec(memory_space=pl.ANY)] * 3,
        [rows_one],
        flops=10**9,
        name="attn_grad",
        placed=False,
    )
    all_d_attn = over_rows(d_attn)
    (d_query,) = call(
        query_grad_kernel,
        [key_work, begins, key_pos, keys, queries, d_attn],
        [SMEM] + [VMEM] * 5,
        [rows_one],
        [pltpu.VMEM((quarter + ROWS, HD), F32)],
        flops=6 * 10**9,
        name="query_grad",
    )
    back_parts = call(
        key_grad_kernel,
        [query_work, starts, query_pos, own_keys, *all_queries, *all_d_attn, d_query, attn],
        [SMEM] + [VMEM] * 13,
        [four] * 4,
        [pltpu.VMEM((LENGTH, HD), BF), pltpu.VMEM((LENGTH, HD), BF), pltpu.VMEM((quarter + ROWS, 2 * HD), F32)]
       ,
        flops=7 * 10**9,
        name="key_grad",
    )
    incoming = output_gradient[0]
    *returning, mixed = call(
        input_grad_kernel,
        [dest, slot, *to_owners(back_parts), pre, dmixed, hist, incoming, w_in],
        [SMEM] * 2 + [VMEM] * 9,
        [shape((2 * BROWS, WIDTH), BF)] * 4 + [shape((ROWS, WIDTH), BF)],
        [
            pltpu.VMEM((ROWS, WIDTH), F32),
            pltpu.VMEM((ROWS, 3 * WIDTH), F32),
            pltpu.VMEM((ROWS, WIDTH), BF),
        ],
        flops=8 * ROWS * WIDTH * WIDTH,
        name="input_grad",
    )
    layer_out, passed = call(
        output_kernel,
        [mixed, hist, w_out, returning[0]],
        [VMEM] * 4,
        [shape((ROWS, WIDTH), BF), shape((2 * BROWS, WIDTH), BF)],
        flops=2 * ROWS * WIDTH * WIDTH,
        name="output",
        placed=False,
    )
    near = [passed] + [send(returning[k], back(chip_pairs(k))) for k in range(1, 4)]
    came_back = near + [send(v, core_pairs()) for v in near]
    (table_grad,) = call(
        table_grad_kernel,
        [dest, row_ids.reshape(1, ROWS), *came_back],
        [SMEM] + [VMEM] * 9,
        [shape((1, 1, tab_rows, WIDTH), BF)],
        [
            pltpu.VMEM((ROWS, WIDTH), BF),
            pltpu.VMEM((tiles, tile, WIDTH), BF),
            pltpu.SemaphoreType.DMA((tiles,)),
        ],
        flops=2 * ROWS * tab_rows * WIDTH,
        name="table_grad",
        out_specs=[pl.BlockSpec(memory_space=pltpu.HBM)],
    )
    return layer_out.reshape(1, ROWS, WIDTH), table_grad


def solution(mesh):
    fine = Mesh(mesh.devices.reshape(4, 4, 4, 2), AXES)
    ctx, tab = ("x", "z"), ("y", "c")
    in_specs = (
        P(ctx, tab, None, None),
        P(ctx, tab, None),
        P(ctx, None, None),
        P(ctx, None, None),
        P(tab, None),
        P(tab, None, None),
        P(),
        P(),
        P(tab, ctx, None),
    )
    out_specs = (P(tab, ctx, None), P(ctx, tab, None, None))
    return jax.shard_map(body, mesh=fine, in_specs=in_specs, out_specs=out_specs, check_vma=False)
```

```python
import functools

import jax
import jax.numpy as jnp
from jax import lax
from jax.experimental import pallas as pl
from jax.experimental.pallas import tpu as pltpu
from jax.sharding import Mesh, PartitionSpec as P

HEADS = 4
BROWS = 64
NBLK = 4
WIDTH = 512
HD = 128
ROWS = 256
CHUNK = 128
LENGTH = 4096
EPS = 1e-05
BF = jnp.bfloat16
F32 = jnp.float32
AXES = ("x", "z", "y", "c")
FAR = 1e9
KEY_TILE = 256
GROUP = 4
KEY_GROUP = 3
SINGLES = 8
ITEMS = 128
SCALE = HD ** (-0.5)


def device_id(x, z, y, c):
    return ((x * 4 + z) * 4 + y) * 2 + c


def all_coords():
    return [(x, z, y, c) for x in range(4) for z in range(4) for y in range(4) for c in range(2)]


def tab_pairs(step):
    out = []
    for x, z, y, c in all_coords():
        y2, c2 = divmod((y * 2 + c + step) % 8, 2)
        out.append((device_id(x, z, y, c), device_id(x, z, y2, c2)))
    return out


def chip_pairs(step):
    return [(device_id(x, z, y, c), device_id(x, z, (y + step) % 4, c)) for x, z, y, c in all_coords()]


def core_pairs():
    return [(device_id(x, z, y, c), device_id(x, z, y, 1 - c)) for x, z, y, c in all_coords()]


def moved(axis, step):
    out = []
    for x, z, y, c in all_coords():
        to = ((x + step) % 4, z) if axis == c else (x, (z + step) % 4)
        out.append((device_id(x, z, y, c), device_id(*to, y, c)))
    return out


def head_pairs(step):
    return moved(0, step)


def row_pairs(step):
    return moved(1, step)


def crossed(values):
    return [values[0], values[2], values[1], values[3]]


def back(pairs):
    return [(b, a) for a, b in pairs]


def send(value, pairs):
    return lax.ppermute(value, AXES, pairs)


def dot(a, b):
    return jnp.dot(a, b, preferred_element_type=F32)


def dot_nt(a, b):
    return lax.dot_general(a, b, (((1,), (1,)), ((), ())), preferred_element_type=F32)


def silu(z):
    h = 0.5 * z
    return h + h * jnp.tanh(h)


def silu_slope(z):
    h = 0.5 * z
    t = jnp.tanh(h)
    return 0.5 * (1.0 + t) * (1.0 + h * (1.0 - t))


def row_statistics(x):
    mean = jnp.mean(x, axis=-1, keepdims=True)
    centred = x - mean
    inverse = lax.rsqrt(jnp.mean(centred * centred, axis=-1, keepdims=True) + EPS)
    return centred * inverse, inverse


def norm_backward(grad, hat, inverse):
    first = jnp.mean(grad, axis=-1, keepdims=True)
    second = jnp.mean(grad * hat, axis=-1, keepdims=True)
    return inverse * (grad - first - hat * second)


def column_of(row):
    return jnp.transpose(jnp.broadcast_to(row, (CHUNK, CHUNK)))


def ds(start, size):
    return pl.ds(pl.multiple_of(start, size), size)


VMEM = pl.BlockSpec(memory_space=pltpu.VMEM)
SMEM = pl.BlockSpec(memory_space=pltpu.SMEM)


def shape(dims, dtype):
    return jax.ShapeDtypeStruct(dims, dtype)


def call(kernel, ins, specs, outs, scratch=(), flops=0, name=None, out_specs=None, limit=40, placed=True):
    moved = sum(a.size * a.dtype.itemsize for a in ins)
    moved += sum(o.size * jnp.dtype(o.dtype).itemsize for o in outs)
    return pl.pallas_call(
        with_place(kernel) if placed else kernel,
        out_shape=outs,
        in_specs=specs,
        out_specs=out_specs or [VMEM] * len(outs),
        scratch_shapes=list(scratch),
        compiler_params=pltpu.CompilerParams(vmem_limit_bytes=limit * 1024 * 1024),
        cost_estimate=pl.CostEstimate(flops=flops, bytes_accessed=moved, transcendentals=0),
        name=name,
    )(*ins)


def with_place(kernel):
    def placed(*refs):
        kernel([lax.axis_index(a) for a in AXES], *refs)

    return placed


def lookup_kernel(meta, dest, ids_ref, table, *rest):
    outs, (buffer, total, column, arrived) = rest[:4], rest[4:]
    tile = buffer.shape[1]
    copies = [
        pltpu.make_async_copy(table.at[0, 0, pl.ds(n * tile, tile), :], buffer.at[n], arrived.at[n])
        for n in range(buffer.shape[0])
    ]
    for copy in copies:
        copy.start()
    for b in range(2):
        column[b * CHUNK : (b + 1) * CHUNK, :] = column_of(ids_ref[b : b + 1, :].astype(F32))
    lane = lax.broadcasted_iota(jnp.int32, (ROWS, CHUNK), 1).astype(F32)
    for n, copy in enumerate(copies):
        hits = [
            jnp.where(column[...] == lane + float(n * tile + m * CHUNK), 1.0, 0.0).astype(BF)
            for m in range(tile // CHUNK)
        ]
        copy.wait()
        part = dot(jnp.concatenate(hits, axis=1), buffer[n])
        if n == 0:
            total[...] = part
        else:
            total[...] += part
    own = meta[2] * 2 + meta[3]
    for k in range(4):
        for core in range(2):
            place = slice(core * BROWS, (core + 1) * BROWS)
            outs[k][place, :] = jnp.zeros((BROWS, WIDTH), BF)
            for p in range(NBLK):

                @pl.when(dest[p, own] == lax.rem(meta[2] + k, 4) * 2 + core)
                def _():
                    outs[k][place, :] = total[p * BROWS : (p + 1) * BROWS, :].astype(BF)


def prepare_kernel(
    meta, lengths, tile_mask, piece, key_work, query_work, starts, begins, key_pos, query_pos, passed, turned, bounds
):
    passed[...] = piece[...]
    row, core = line(meta)[1], meta[3]
    ends, end = [], jnp.int32(0)
    for d in range(lengths.shape[0]):
        end = end + lengths[d]
        ends.append(end)
    for t in range(8):
        i = chunk_of(t, row, core)
        begin, stop = jnp.int32(0), jnp.int32(LENGTH)
        for end in ends:
            begin = jnp.where(i * CHUNK >= end, end, begin)
        for end in reversed(ends):
            stop = jnp.where(i * CHUNK + CHUNK - 1 < end, end, stop)
        bounds[t] = begin
        bounds[8 + t] = stop - 1

    def key_span(t):
        i = chunk_of(t, row, core)
        return bounds[t] // KEY_TILE, (i * CHUNK + CHUNK - 1) // KEY_TILE

    def query_span(t):
        i = chunk_of(t, row, core)
        return (i * CHUNK) // KEY_TILE, bounds[8 + t] // KEY_TILE

    list_work(key_work, key_span, core)
    list_work(query_work, query_span, core)
    turned[...] = jnp.transpose(tile_mask[...].astype(F32))
    on_keys, on_queries = [], []
    for t in range(8):
        i = chunk_of(t, row, core)
        position = lax.broadcasted_iota(jnp.int32, (CHUNK, CHUNK), 0) + i * CHUNK
        begin = jnp.zeros((CHUNK, CHUNK), jnp.int32)
        for end in ends:
            begin = jnp.where(position >= end, end, begin)
        begins[t * CHUNK : (t + 1) * CHUNK, :] = begin.astype(F32)
        for m in range(2):
            on_keys.append(tile_mask[pl.ds(2 * i + m, 1), :])
            on_queries.append(turned[pl.ds(2 * i + m, 1), :])
    on_keys = jnp.concatenate(on_keys, axis=0).astype(F32).astype(BF)
    on_queries = jnp.concatenate(on_queries, axis=0).astype(BF)
    for n in range(8):
        cols = slice(n * WIDTH, (n + 1) * WIDTH)
        spot = lax.broadcasted_iota(jnp.int32, (BROWS, WIDTH), 1) + n * WIDTH
        pick = jnp.where(
            lax.broadcasted_iota(jnp.int32, (BROWS, WIDTH), 0) == spot // BROWS, 1.0, 0.0
        ).astype(BF)
        spot = spot[0:16, :]
        place = spot.astype(F32)
        key_pos[:, cols] = jnp.where(dot(on_keys, pick) > 0.5, place, FAR)
        query_pos[:, cols] = jnp.where(dot(on_queries, pick) > 0.5, place, -1.0)
        spot = spot[0:8, :]
        begin = jnp.zeros((8, WIDTH), jnp.int32)
        for end in ends:
            begin = jnp.where(spot >= end, end, begin)
        starts[:, cols] = begin.astype(F32)


def mix_kernel(incoming, w_out, dmixed):
    dmixed[...] = dot_nt(incoming[...], w_out[...])


def project_kernel(meta, dest, slot, *rest):
    blocks, (w_ref, dmixed_ref), rest = rest[:8], rest[8:10], rest[10:]
    hist, pre = rest[:2]
    outs = rest[2:6]
    act, grads = rest[6:]
    core = meta[3]
    own = meta[2] * 2 + core
    for k in range(8):
        source = lax.rem(meta[2] - k % 4 + 4, 4) * 2 + (core if k < 4 else 1 - core)
        for p in range(NBLK):

            @pl.when(dest[p, source] == own)
            def _():
                hist[ds(slot[p, source] * BROWS, BROWS), :] = blocks[k][ds(core * BROWS, BROWS), :]

    hat, _ = row_statistics(hist[...].astype(F32))
    normed = hat.astype(BF)
    for n in range(4):
        cols = slice(n * WIDTH, (n + 1) * WIDTH)
        part = dot(normed, w_ref[:, cols])
        pre[:, cols] = part
        act[:, cols] = silu(part).astype(BF)
    grads[...] = (dmixed_ref[...] * act[:, 0:WIDTH].astype(F32)).astype(BF)
    for j in range(4):
        head = lax.rem(line(meta)[0] + j, 4) * HD
        outs[j][:, 0:HD] = act[:, ds(3 * WIDTH + head, HD)]
        outs[j][:, HD : 2 * HD] = act[:, ds(WIDTH + head, HD)]
        outs[j][:, 2 * HD : 3 * HD] = act[:, ds(2 * WIDTH + head, HD)]
        outs[j][:, 3 * HD : 4 * HD] = grads[:, ds(head, HD)]


def line(meta):
    first = meta[3] == 0
    return jnp.where(first, meta[0], meta[1]), jnp.where(first, meta[1], meta[0])


def chunk_of(t, row, core):
    spread = 4 * t + jnp.where(t < 4, row, 3 - row)
    solid = t + jnp.where(t < 4, 4 * row, 24 - 4 * row)
    return jnp.where(core == 0, spread, solid)


def pieces_of(meta):
    head = line(meta)[0]
    for j in range(4):
        source = lax.rem(head - j + 4, 4)
        yield j, 0, source
        yield j, CHUNK, 7 - source


def collect_kernel(meta, p0, p2, p1, p3, keys, queries, grads):
    pieces = (p0, p1, p2, p3)
    for j, low, t in pieces_of(meta):
        rows, part = ds(t * CHUNK, CHUNK), pieces[j]
        keys[rows, :] = part[low : low + CHUNK, 0 : 2 * HD]
        queries[rows, :] = part[low : low + CHUNK, 2 * HD : 3 * HD]
        grads[rows, :] = part[low : low + CHUNK, 3 * HD : 4 * HD]


def place_rows(meta, parts, out):
    row, core = line(meta)[1], meta[3]
    for k in range(4):
        other = lax.rem(row - k + 4, 4)
        for t in range(8):
            chunk = chunk_of(t, other, core)
            out[ds(chunk * CHUNK, CHUNK), :] = parts[k][t * CHUNK : (t + 1) * CHUNK, :]


def list_work(work, span, core):
    def put(unit):
        def one(n, count):
            work[count] = unit
            work[ITEMS + count] = n
            return count + 1

        return one

    def one_pair(p, count):
        low, high = span(2 * p)
        low_next, high_next = span(2 * p + 1)

        def together(count):
            count = lax.fori_loop(low, high + 1, put(p), count)
            return lax.fori_loop(jnp.maximum(low_next, high + 1), high_next + 1, put(p), count)

        def alone(count):
            count = lax.fori_loop(low, high + 1, put(2 * p), count)
            return lax.fori_loop(low_next, high_next + 1, put(2 * p + 1), count)

        return lax.cond(core == 0, alone, together, count)

    count = lax.fori_loop(0, 4, one_pair, jnp.int32(0))
    for u in range(SINGLES):
        work[count + u] = jnp.where(core == 0, 8, 4)
        work[ITEMS + count + u] = 0
    work[2 * ITEMS] = count


def run_items(work, core, item, size):
    def run(group_size, rows, last):
        def group(b, carry):
            done = []
            for u in range(group_size):
                slot, n = work[b * group_size + u], work[ITEMS + b * group_size + u]
                done.append((slot, item(jnp.minimum(slot, last), n, rows)))
            for slot, parts in done:
                for ref, cols, part in parts:
                    ref[ds(slot * rows, rows), cols] += part
            return carry

        lax.fori_loop(0, (work[2 * ITEMS] + group_size - 1) // group_size, group, 0)

    @pl.when(core == 0)
    def _():
        run(SINGLES, CHUNK, 7)

    @pl.when(core != 0)
    def _():
        run(size, ROWS, 3)


def unit_positions(meta, unit, rows, width):
    row, core = line(meta)[1], meta[3]
    local = lax.broadcasted_iota(jnp.int32, (CHUNK, width), 0).astype(F32)
    count = rows // CHUNK
    return jnp.concatenate(
        [local + (chunk_of(count * unit + m, row, core) * CHUNK).astype(F32) for m in range(count)], axis=0
    )


def spread_rows(table, unit, rows, cols):
    count = rows // BROWS
    return jnp.concatenate(
        [jnp.broadcast_to(table[pl.ds(count * unit + m, 1), cols], (BROWS, KEY_TILE)) for m in range(count)],
        axis=0,
    )


def allowed_keys(meta, begins, key_pos, unit, n, rows):
    repeat = KEY_TILE // CHUNK
    pos = jnp.concatenate([unit_positions(meta, unit, rows, CHUNK)] * repeat, axis=1)
    start = jnp.concatenate([begins[ds(unit * rows, rows), :]] * repeat, axis=1)
    key = spread_rows(key_pos, unit, rows, ds(n * KEY_TILE, KEY_TILE))
    return (key >= start) & (key <= pos)


def forward_kernel(
    meta, work, begins, key_pos, k0, k2, k1, k3, queries, grads, keys, attn, stats, total
):
    place_rows(meta, (k0, k1, k2, k3), keys)
    total[...] = jnp.zeros_like(total)

    def item(unit, n, rows):
        near = ds(n * KEY_TILE, KEY_TILE)
        h = dot_nt(queries[ds(unit * rows, rows), :], keys[near, 0:HD]) * (0.5 * SCALE)
        allowed = allowed_keys(meta, begins, key_pos, unit, n, rows)
        probs = jnp.where(allowed, h + h * jnp.tanh(h), 0.0).astype(BF)
        return [(total, slice(None), dot(probs, keys[near, HD : 2 * HD]))]

    run_items(work, meta[3], item, GROUP)
    lane = lax.broadcasted_iota(jnp.int32, (CHUNK, CHUNK), 1)
    for t in range(8):
        rows = slice(t * CHUNK, (t + 1) * CHUNK)
        x = total[rows, :]
        attn[rows, :] = x
        e = grads[rows, :].astype(F32)
        mean = jnp.mean(x, axis=1, keepdims=True)
        centred = x - mean
        packed = jnp.where(lane == 0, mean, 0.0)
        packed = jnp.where(lane == 1, jnp.sum(centred * centred, axis=1, keepdims=True), packed)
        packed = jnp.where(lane == 2, jnp.sum(e, axis=1, keepdims=True), packed)
        packed = jnp.where(lane == 3, jnp.sum(e * centred, axis=1, keepdims=True), packed)
        stats[:, rows] = jnp.transpose(packed)[0:8, :]


def attn_grad_kernel(s0, s1, s2, s3, attn, grads, q1, q2, q3, out):
    parts = [s[...] for s in (s0, s1, s2, s3)]
    means = [s[0:1, :] for s in parts]
    mean = (means[0] + means[1] + means[2] + means[3]) * 0.25
    spread = sum(s[1:2, :] + HD * (m - mean) * (m - mean) for s, m in zip(parts, means))
    inverse = lax.rsqrt(spread * (1.0 / WIDTH) + EPS)
    e_mean = sum(s[2:3, :] for s in parts) * (1.0 / WIDTH)
    e_on = sum(s[3:4, :] + (m - mean) * s[2:3, :] for s, m in zip(parts, means))
    e_on = e_on * inverse * (1.0 / WIDTH)
    for t in range(8):
        rows = slice(t * CHUNK, (t + 1) * CHUNK)
        cols = [column_of(v[:, rows]) for v in (mean, inverse, e_mean, e_on)]
        hat = (attn[rows, :] - cols[0]) * cols[1]
        out[rows, :] = (cols[1] * (grads[rows, :].astype(F32) - cols[2] - hat * cols[3])).astype(BF)


def query_grad_kernel(meta, work, begins, key_pos, keys, queries, d_attn, out, total):
    total[...] = jnp.zeros_like(total)

    def item(unit, n, rows):
        near = ds(n * KEY_TILE, KEY_TILE)
        own = ds(unit * rows, rows)
        k = keys[near, 0:HD]
        h = dot_nt(queries[own, :], k) * (0.5 * SCALE)
        dp = dot_nt(d_attn[own, :], keys[near, HD : 2 * HD])
        th = jnp.tanh(h)
        allowed = allowed_keys(meta, begins, key_pos, unit, n, rows)
        d_scores = jnp.where(allowed, dp * ((1.0 + th) * (1.0 + h - h * th)), 0.0)
        return [(total, slice(None), dot(d_scores.astype(BF), k))]

    run_items(work, meta[3], item, GROUP)
    out[...] = (total[0 : LENGTH // 4, :] * (0.5 * SCALE)).astype(BF)


def key_grad_kernel(
    meta, work, starts, query_pos, keys, q0, q2, q1, q3, g0, g2, g1, g3, d_query, attn,
    r0, r1, r2, r3, queries, grads, total,
):
    outs = (r0, r1, r2, r3)
    place_rows(meta, (q0, q1, q2, q3), queries)
    place_rows(meta, (g0, g1, g2, g3), grads)
    total[...] = jnp.zeros_like(total)

    def item(unit, n, rows):
        own = ds(unit * rows, rows)
        near = ds(n * KEY_TILE, KEY_TILE)
        q, g = queries[near, :], grads[near, :]
        pos = unit_positions(meta, unit, rows, KEY_TILE)
        begin = jnp.broadcast_to(starts[0:1, near], (rows, KEY_TILE))
        allowed = (pos <= spread_rows(query_pos, unit, rows, near)) & (pos >= begin)
        h = dot_nt(keys[own, 0:HD], q) * (0.5 * SCALE)
        dp = dot_nt(keys[own, HD : 2 * HD], g)
        th = jnp.tanh(h)
        up = 1.0 + th
        probs = jnp.where(allowed, h * up, 0.0).astype(BF)
        d_scores = jnp.where(allowed, dp * (up * (1.0 + h - h * th)), 0.0).astype(BF)
        return [
            (total, slice(0, HD), dot(d_scores, q)),
            (total, slice(HD, 2 * HD), dot(probs, g)),
        ]

    run_items(work, meta[3], item, KEY_GROUP)
    for j, low, t in pieces_of(meta):
        rows = ds(t * CHUNK, CHUNK)
        outs[j][low : low + CHUNK, 0:HD] = (total[rows, 0:HD] * (0.5 * SCALE)).astype(BF)
        outs[j][low : low + CHUNK, HD : 2 * HD] = total[rows, HD : 2 * HD].astype(BF)
        outs[j][low : low + CHUNK, 2 * HD : 3 * HD] = d_query[rows, :]
        outs[j][low : low + CHUNK, 3 * HD : 4 * HD] = attn[rows, :].astype(BF)


def input_grad_kernel(meta, dest, slot, p0, p2, p1, p3, pre, dmixed, hist, incoming, w_in, *rest):
    outs, (mixed, attn, d_act, result) = rest[:4], rest[4:]
    for j, part in enumerate((p0, p1, p2, p3)):
        head = lax.rem(line(meta)[0] + j, 4) * HD
        d_act[:, ds(2 * WIDTH + head, HD)] = part[:, 0:HD].astype(F32)
        d_act[:, ds(head, HD)] = part[:, HD : 2 * HD].astype(F32)
        d_act[:, ds(WIDTH + head, HD)] = part[:, 2 * HD : 3 * HD].astype(F32)
        attn[:, ds(head, HD)] = part[:, 3 * HD : 4 * HD].astype(F32)
    on, _ = row_statistics(attn[...])
    u_pre = pre[:, 0:WIDTH]
    mixed[...] = (on * silu(u_pre).astype(BF).astype(F32)).astype(BF)
    total = dot_nt((dmixed[...] * on * silu_slope(u_pre)).astype(BF), w_in[:, 0:WIDTH])
    for n in range(3):
        cols = slice((n + 1) * WIDTH, (n + 2) * WIDTH)
        d_pre = (d_act[:, n * WIDTH : (n + 1) * WIDTH] * silu_slope(pre[:, cols])).astype(BF)
        total = total + dot_nt(d_pre, w_in[:, cols])
    hat, inverse = row_statistics(hist[...].astype(F32))
    result[...] = (incoming[...].astype(F32) + norm_backward(total, hat, inverse)).astype(BF)
    own = meta[2] * 2 + meta[3]
    for k in range(4):
        for core in range(2):
            place = slice(core * BROWS, (core + 1) * BROWS)
            outs[k][place, :] = jnp.zeros((BROWS, WIDTH), BF)
            source = lax.rem(meta[2] - k + 4, 4) * 2 + core
            for p in range(NBLK):

                @pl.when(dest[p, source] == own)
                def _():
                    outs[k][place, :] = result[ds(slot[p, source] * BROWS, BROWS), :]


def output_kernel(mixed, hist, w_out, block, out, passed):
    passed[...] = block[...]
    out[...] = (hist[...].astype(F32) + dot(mixed[...], w_out[...])).astype(BF)


def table_grad_kernel(meta, dest, ids, *rest):
    blocks, out, rows, buffer, sent = rest[:8], rest[8], rest[9], rest[10], rest[11]
    tile = buffer.shape[1]
    core = meta[3]
    own = meta[2] * 2 + core
    for k in range(8):
        owner = lax.rem(meta[2] + k % 4, 4) * 2 + (core if k < 4 else 1 - core)
        for p in range(NBLK):

            @pl.when(dest[p, own] == owner)
            def _():
                rows[p * BROWS : (p + 1) * BROWS, :] = blocks[k][ds(core * BROWS, BROWS), :]

    number = lax.broadcasted_iota(jnp.int32, (tile, ROWS), 0)
    copies = []
    for n in range(buffer.shape[0]):
        hits = jnp.where(number + n * tile == ids[...], 1.0, 0.0).astype(BF)
        buffer[n] = dot(hits, rows[...]).astype(BF)
        copy = pltpu.make_async_copy(buffer.at[n], out.at[0, 0, pl.ds(n * tile, tile), :], sent.at[n])
        copy.start()
        copies.append(copy)
    for copy in copies:
        copy.wait()


def body(table, row_ids, dests, slots, lengths, tile_mask, w_in, w_out, output_gradient):
    dest = dests[0].T
    slot = slots[0].T
    tab_rows = table.shape[2]

    tiles = 8
    tile = tab_rows // tiles
    block_shape = shape((BROWS, WIDTH), BF)
    outgoing = call(
        lookup_kernel,
        [dest, row_ids.reshape(2, CHUNK), table],
        [SMEM, VMEM, pl.BlockSpec(memory_space=pltpu.HBM)],
        [shape((2 * BROWS, WIDTH), BF)] * 4,
        [
            pltpu.VMEM((tiles, tile, WIDTH), BF),
            pltpu.VMEM((ROWS, WIDTH), F32),
            pltpu.VMEM((ROWS, CHUNK), F32),
            pltpu.SemaphoreType.DMA((tiles,)),
        ],
        flops=2 * ROWS * tab_rows * WIDTH,
        name="lookup",
        limit=60,
    )
    near = [outgoing[0]] + [send(outgoing[k], chip_pairs(k)) for k in range(1, 4)]
    blocks = near + [send(v, core_pairs()) for v in near]

    (dmixed,) = call(
        mix_kernel,
        [output_gradient[0], w_out],
        [VMEM] * 2,
        [shape((ROWS, WIDTH), F32)],
        flops=10**9,
        name="mix",
        placed=False,
    )

    four = shape((ROWS, 4 * HD), BF)
    two = shape((ROWS, 2 * HD), BF)
    one = shape((ROWS, HD), BF)
    quarter = LENGTH // 4
    rows_two = shape((quarter, 2 * HD), BF)
    rows_one = shape((quarter, HD), BF)

    def to_heads(values):
        return [values[0]] + [send(values[j], head_pairs(j)) for j in range(1, 4)]

    def to_owners(values):
        return [values[0]] + [send(values[j], back(head_pairs(j))) for j in range(1, 4)]

    def over_rows(value):
        return [value] + [send(value, row_pairs(k)) for k in range(1, 4)]

    hist, pre, *pieces = call(
        project_kernel,
        [dest, slot, *blocks, w_in, dmixed],
        [SMEM] * 2 + [VMEM] * 10,
        [shape((ROWS, WIDTH), BF), shape((ROWS, 4 * WIDTH), F32)] + [four] * 4,
        [pltpu.VMEM((ROWS, 4 * WIDTH), BF), pltpu.VMEM((ROWS, WIDTH), BF)],
        flops=2 * ROWS * WIDTH * 4 * WIDTH,
        name="project",
    )
    key_work, query_work, starts, begins, key_pos, query_pos, passed = call(
        prepare_kernel,
        [lengths[0], tile_mask[0], pieces[0]],
        [SMEM] + [VMEM] * 2,
        [
            shape((2 * ITEMS + 1,), jnp.int32),
            shape((2 * ITEMS + 1,), jnp.int32),
            shape((8, LENGTH), F32),
            shape((LENGTH // 4, CHUNK), F32),
            shape((16, LENGTH), F32),
            shape((16, LENGTH), F32),
            four,
        ],
        [pltpu.VMEM((64, 64), F32), pltpu.SMEM((16,), jnp.int32)],
        flops=3 * 10**9,
        name="prepare",
        out_specs=[SMEM] * 2 + [VMEM] * 5,
    )

    own_keys, queries, grads = call(
        collect_kernel,
        crossed([passed, *to_heads(pieces)[1:]]),
        [VMEM] * 4,
        [rows_two, rows_one, rows_one],
        name="collect",
    )
    keys, attn, stats = call(
        forward_kernel,
        [key_work, begins, key_pos, *crossed(over_rows(own_keys)), queries, grads],
        [SMEM] + [VMEM] * 8,
        [shape((LENGTH, 2 * HD), BF), shape((quarter, HD), F32), shape((8, quarter), F32)],
        [pltpu.VMEM((quarter + ROWS, HD), F32)],
        flops=6 * 10**9,
        name="forward",
    )
    all_queries = over_rows(queries)
    (d_attn,) = call(
        attn_grad_kernel,
        [*crossed(to_heads([stats] * 4)), attn, grads, *all_queries[1:]],
        [VMEM] * 6 + [pl.BlockSpec(memory_space=pl.ANY)] * 3,
        [rows_one],
        flops=10**9,
        name="attn_grad",
        placed=False,
    )
    all_d_attn = over_rows(d_attn)
    (d_query,) = call(
        query_grad_kernel,
        [key_work, begins, key_pos, keys, queries, d_attn],
        [SMEM] + [VMEM] * 5,
        [rows_one],
        [pltpu.VMEM((quarter + ROWS, HD), F32)],
        flops=6 * 10**9,
        name="query_grad",
    )
    back_parts = call(
        key_grad_kernel,
        [query_work, starts, query_pos, own_keys, *crossed(all_queries), *crossed(all_d_attn), d_query, attn],
        [SMEM] + [VMEM] * 13,
        [four] * 4,
        [pltpu.VMEM((LENGTH, HD), BF), pltpu.VMEM((LENGTH, HD), BF), pltpu.VMEM((quarter + ROWS, 2 * HD), F32)]
       ,
        flops=7 * 10**9,
        name="key_grad",
    )
    incoming = output_gradient[0]
    *returning, mixed = call(
        input_grad_kernel,
        [dest, slot, *crossed(to_owners(back_parts)), pre, dmixed, hist, incoming, w_in],
        [SMEM] * 2 + [VMEM] * 9,
        [shape((2 * BROWS, WIDTH), BF)] * 4 + [shape((ROWS, WIDTH), BF)],
        [
            pltpu.VMEM((ROWS, WIDTH), F32),
            pltpu.VMEM((ROWS, 3 * WIDTH), F32),
            pltpu.VMEM((ROWS, WIDTH), BF),
        ],
        flops=8 * ROWS * WIDTH * WIDTH,
        name="input_grad",
    )
    layer_out, passed = call(
        output_kernel,
        [mixed, hist, w_out, returning[0]],
        [VMEM] * 4,
        [shape((ROWS, WIDTH), BF), shape((2 * BROWS, WIDTH), BF)],
        flops=2 * ROWS * WIDTH * WIDTH,
        name="output",
        placed=False,
    )
    near = [passed] + [send(returning[k], back(chip_pairs(k))) for k in range(1, 4)]
    came_back = near + [send(v, core_pairs()) for v in near]
    (table_grad,) = call(
        table_grad_kernel,
        [dest, row_ids.reshape(1, ROWS), *came_back],
        [SMEM] + [VMEM] * 9,
        [shape((1, 1, tab_rows, WIDTH), BF)],
        [
            pltpu.VMEM((ROWS, WIDTH), BF),
            pltpu.VMEM((tiles, tile, WIDTH), BF),
            pltpu.SemaphoreType.DMA((tiles,)),
        ],
        flops=2 * ROWS * tab_rows * WIDTH,
        name="table_grad",
        out_specs=[pl.BlockSpec(memory_space=pltpu.HBM)],
    )
    return layer_out.reshape(1, ROWS, WIDTH), table_grad


def solution(mesh):
    fine = Mesh(mesh.devices.reshape(4, 4, 4, 2), AXES)
    ctx, tab = ("x", "z"), ("y", "c")
    in_specs = (
        P(ctx, tab, None, None),
        P(ctx, tab, None),
        P(ctx, None, None),
        P(ctx, None, None),
        P(tab, None),
        P(tab, None, None),
        P(),
        P(),
        P(tab, ctx, None),
    )
    out_specs = (P(tab, ctx, None), P(ctx, tab, None, None))
    return jax.shard_map(body, mesh=fine, in_specs=in_specs, out_specs=out_specs, check_vma=False)
```
